32 devices in a mesh: line: 4 (over y, x), stream: 4 (over z), span: 2 (over core).
Axes of the slice: x: 2, y: 2, z: 4, core: 2. Of those that a mesh axis runs over, the one named last changes fastest.
Arguments:
- velocity: float32 [3, 256, 16, 512], P(None, 'line', 'span', 'stream'), may hold values from -6 to 6
- cotangent: float32 [3, 256, 16, 512], P(None, 'line', 'span', 'stream'), may hold values from -6 to 6
- in_weight: bfloat16 [2048, 128], replicated, may hold values from -0.5 to 0.5
- in_bias: float32 [2048], replicated, may hold values from -3 to 3
- out_weight: bfloat16 [3, 2048], replicated, may hold values from -0.125 to 0.125
- diffusion: float32 [256], replicated, may hold values from 1000 to 10000
- stencil: int32 [2, 128], replicated, may hold values from 0 to 23
- wall_mask: int32 [2, 16, 512], P(None, 'span', 'stream'), may hold values 0 or 1
Outputs:
- new_velocity: float32 [3, 256, 16, 512], P(None, 'line', 'span', 'stream')
- adjoint_velocity: float32 [3, 256, 16, 512], P(None, 'line', 'span', 'stream')
- grad_in_weight: float32 [2048, 128], P('line')
- grad_in_bias: float32 [2048], P('line')
- grad_out_weight: float32 [3, 2048], P(None, 'line')
The draws below stay inside these ranges and needn't reach their ends.
Inputs may be any that keep to these rules, and one draw needn't show every extreme that they name: stencil[w, f] reads component stencil[w, f] // 8 at stencil[w, f] % 8 rows from wall w.
All inputs are finite; a program needn't handle non-finite values. No bound on the sum of `wall_mask` on one device may be relied on, other than what follows from the above.
Results may differ from the reference program's by a relative error of at most 0.012.
Values sent between devices are 32-bit elements; how exact they have to be, the bound alone decides.
A program may use at most 64 MiB of HBM per device.

```python
import math
import jax
import jax.numpy as jnp
from jax import lax

F = 128
H = 2048
WALL_ROWS = 8
NY = 256
NZ = 16
NX = 512


def plant(array, key, low, largest):
    shape = array.shape
    place = [jax.random.randint(jax.random.fold_in(key, axis), (), 0, shape[axis]) for axis in range(len(shape))]
    array = array.at[tuple(place)].set(low)
    longest = shape.index(max(shape))
    place[longest] = (place[longest] + 1) % shape[longest]
    return array.at[tuple(place)].set(largest)


def level_of(stream_key, shape, split, low, top_value):
    def one(dim, blocks):
        steps = jax.random.uniform(jax.random.fold_in(jax.random.fold_in(stream_key, 6), dim), (blocks,), jnp.float32, low / len(split), top_value / len(split))
        return jnp.repeat(jnp.exp(steps), shape[dim] // blocks).reshape((-1,) + (1,) * (len(shape) - dim - 1))

    loudness = one(*split[0])
    for cut in split[1:]:
        loudness = loudness * one(*cut)
    return loudness


def normal_values(key, shape, spread, reach, shards=(), dtype=jnp.bfloat16):
    loudness = level_of(key, shape, shards, -0.22, 0.18) if shards else 1.0
    values = jax.random.normal(key, shape, jnp.float32) * spread * loudness
    return jnp.minimum(jnp.maximum(values, -reach), reach).astype(dtype)


def setup_inputs(seed: int = 0) -> dict:
    key_list = jax.random.split(jax.random.key(seed), 9)
    velocity = normal_values(key_list[0], (3, NY, NZ, NX), 1.0, 6.0, ((1, 4), (2, 2), (3, 4)), jnp.float32)
    cotangent = normal_values(key_list[1], (3, NY, NZ, NX), 1.0, 6.0, ((1, 4), (2, 2), (3, 4)), jnp.float32)
    in_weight = normal_values(key_list[2], (H, F), F ** -0.5, 0.5)
    in_bias = normal_values(key_list[3], (H,), 0.5, 3.0, (), jnp.float32)
    out_weight = normal_values(key_list[4], (3, H), H ** -0.5, 0.125)
    diffusion = jnp.clip(jnp.exp(jax.random.uniform(key_list[5], (NY,), jnp.float32, math.log(1000.0), math.log(10000.0))), 1000.0, 10000.0)
    stencil = plant(jax.random.randint(key_list[6], (2, F), 0, 3 * WALL_ROWS), jax.random.fold_in(key_list[6], 1), 0, (3 * WALL_ROWS) - 1).astype(jnp.int32)
    wall_mask = plant((jax.random.randint(key_list[7], (2, NZ, NX), 0, 4) < 3).astype(jnp.int32), jax.random.fold_in(key_list[7], 1), 0, 1)
    return {"velocity": velocity, "cotangent": cotangent, "in_weight": in_weight, "in_bias": in_bias, "out_weight": out_weight, "diffusion": diffusion, "stencil": stencil, "wall_mask": wall_mask}


ADVECT = 0.2


def thomas(sub_coef, main_coef, sup_coef, rhs):
    def forward(carried, row_data):
        ratio_prev, reduced_prev = carried
        sub_val, main_val, sup_val, rhs_row = row_data
        divisor = main_val - sub_val * ratio_prev
        ratio_new = sup_val / divisor
        reduced_new = (rhs_row - sub_val * reduced_prev) / divisor
        return (ratio_new, reduced_new), (ratio_new, reduced_new)

    start = (jnp.zeros((), jnp.float32), jnp.zeros(rhs.shape[1:], jnp.float32))
    _, (ratio_all, reduced_all) = lax.scan(forward, start, (sub_coef, main_coef, sup_coef, rhs))

    def backward(value_next, row_data):
        ratio_row, reduced_row = row_data
        value_row = reduced_row - ratio_row * value_next
        return value_row, value_row

    _, solved = lax.scan(backward, jnp.zeros(rhs.shape[1:], jnp.float32), (ratio_all, reduced_all), reverse=True)
    return solved


def closure_forward(wall_slab, pick_rows, mask_float, in_weight, in_bias, out_weight):
    features = jnp.take(wall_slab, pick_rows, axis=0).astype(jnp.bfloat16)
    feature_planes = jnp.transpose(features, (1, 0, 2))

    def one_plane(plane_feats):
        hidden = jnp.tanh(jnp.dot(in_weight, plane_feats, preferred_element_type=jnp.float32) + in_bias[:, None]).astype(jnp.bfloat16)
        return hidden, jnp.dot(out_weight, hidden, preferred_element_type=jnp.float32)

    hidden_planes, stress_planes = lax.map(one_plane, feature_planes)
    stress = jnp.transpose(stress_planes, (1, 0, 2)) * mask_float[None]
    return feature_planes, hidden_planes, stress


def closure_backward(totals, feature_planes, hidden_planes, stress_grad, pick_rows, in_weight, out_weight):
    grad_planes = jnp.transpose(stress_grad, (1, 0, 2))

    def closure_back(running, plane_data):
        plane_feats, hidden, plane_grad = plane_data
        grad_out = running[2] + lax.dot_general(plane_grad, hidden, (((1,), (1,)), ((), ())), preferred_element_type=jnp.float32)
        hidden_grad = lax.dot_general(out_weight, plane_grad, (((0,), (0,)), ((), ())), preferred_element_type=jnp.float32)
        hidden_float = hidden.astype(jnp.float32)
        pre_grad = (hidden_grad * (1.0 - hidden_float * hidden_float)).astype(jnp.bfloat16)
        grad_in = running[0] + lax.dot_general(pre_grad, plane_feats, (((1,), (1,)), ((), ())), preferred_element_type=jnp.float32)
        grad_bias = running[1] + jnp.sum(pre_grad.astype(jnp.float32), axis=1)
        feature_grad = lax.dot_general(in_weight, pre_grad, (((0,), (0,)), ((), ())), preferred_element_type=jnp.float32)
        return (grad_in, grad_bias, grad_out), feature_grad

    totals, feature_grads = lax.scan(closure_back, totals, (feature_planes, hidden_planes, grad_planes))
    selector = (pick_rows[:, None] == jnp.arange(3 * WALL_ROWS)[None, :]).astype(jnp.float32)
    slab_grad = jnp.einsum("fk,zfx->kzx", selector, feature_grads, precision=lax.Precision.HIGHEST)
    return totals, slab_grad


def reference(velocity, cotangent, in_weight, in_bias, out_weight, diffusion, stencil, wall_mask):
    row_count = velocity.shape[1]
    above_all = jnp.concatenate([diffusion[1:], diffusion[-1:]])
    sub_coef = -diffusion
    sup_coef = -above_all
    main_coef = 1.0 + diffusion + above_all

    def solve_lines(rhs):
        return jnp.moveaxis(thomas(sub_coef, main_coef, sup_coef, jnp.moveaxis(rhs, 1, 0)), 0, 1)

    grad_stream = jnp.roll(velocity, -1, axis=3) - jnp.roll(velocity, 1, axis=3)
    grad_span = jnp.roll(velocity, -1, axis=2) - jnp.roll(velocity, 1, axis=2)
    explicit = velocity - ADVECT * (velocity[0] * grad_stream + velocity[2] * grad_span)

    slab_bottom = velocity[:, :WALL_ROWS].reshape(3 * WALL_ROWS, NZ, NX)
    slab_top = velocity[:, row_count - WALL_ROWS:][:, ::-1].reshape(3 * WALL_ROWS, NZ, NX)
    mask_bottom = wall_mask[0].astype(jnp.float32)
    mask_top = wall_mask[1].astype(jnp.float32)
    feats_bottom, hidden_bottom, stress_bottom = closure_forward(slab_bottom, stencil[0], mask_bottom, in_weight, in_bias, out_weight)
    feats_top, hidden_top, stress_top = closure_forward(slab_top, stencil[1], mask_top, in_weight, in_bias, out_weight)
    rhs = explicit.at[:, 0].add(stress_bottom).at[:, row_count - 1].add(stress_top)
    new_velocity = solve_lines(rhs)

    multiplier = solve_lines(cotangent)
    grad_bottom = (multiplier[:, 0] * mask_bottom[None]).astype(jnp.bfloat16)
    grad_top = (multiplier[:, row_count - 1] * mask_top[None]).astype(jnp.bfloat16)
    totals = (jnp.zeros(in_weight.shape, jnp.float32), jnp.zeros(in_bias.shape, jnp.float32), jnp.zeros(out_weight.shape, jnp.float32))
    totals, slab_grad_bottom = closure_backward(totals, feats_bottom, hidden_bottom, grad_bottom, stencil[0], in_weight, out_weight)
    totals, slab_grad_top = closure_backward(totals, feats_top, hidden_top, grad_top, stencil[1], in_weight, out_weight)

    flux_stream = velocity[0] * multiplier
    flux_span = velocity[2] * multiplier
    adjoint = multiplier + ADVECT * ((jnp.roll(flux_stream, -1, axis=3) - jnp.roll(flux_stream, 1, axis=3)) + (jnp.roll(flux_span, -1, axis=2) - jnp.roll(flux_span, 1, axis=2)))
    adjoint = adjoint.at[0].add(-ADVECT * jnp.sum(multiplier * grad_stream, axis=0))
    adjoint = adjoint.at[2].add(-ADVECT * jnp.sum(multiplier * grad_span, axis=0))
    adjoint = adjoint.at[:, :WALL_ROWS].add(slab_grad_bottom.reshape(3, WALL_ROWS, NZ, NX))
    adjoint = adjoint.at[:, row_count - WALL_ROWS:].add(slab_grad_top.reshape(3, WALL_ROWS, NZ, NX)[:, ::-1])
    return new_velocity, adjoint, totals[0], totals[1], totals[2]
```

```python
import jax
import jax.numpy as jnp
from jax import lax
from jax.experimental import pallas as pl
from jax.experimental.pallas import tpu as pltpu
from jax.sharding import PartitionSpec as P

WALL_ROWS = 8
ADVECT = 0.2
HIGHEST = lax.Precision.HIGHEST


def prefix_kernel(step_ref, start_ref, end_ref, out_ref, total_ref):
    step = step_ref[...]
    count = step.shape[1]
    lane = lax.broadcasted_iota(jnp.int32, step.shape, 1)
    head = lane == 0
    one = jnp.ones_like(step)
    zero = jnp.zeros_like(step)
    a, b = one, jnp.where(head, zero, step)
    c, d = jnp.where(head, zero, one), jnp.where(head, one, one + step)
    hop = 1
    while hop < count:
        keep = lane >= hop
        pa = jnp.where(keep, pltpu.roll(a, hop, 1), one)
        pb = jnp.where(keep, pltpu.roll(b, hop, 1), zero)
        pc = jnp.where(keep, pltpu.roll(c, hop, 1), zero)
        pd = jnp.where(keep, pltpu.roll(d, hop, 1), one)
        a, b, c, d = a * pa + b * pc, a * pb + b * pd, c * pa + d * pc, c * pb + d * pd
        hop *= 2
    flux = start_ref[...] + 1.0
    value = a + b * flux
    out_ref[...] = value
    total_ref[...] = c + d * flux + end_ref[...] * value


def green_factors(diffusion):
    count = diffusion.shape[0]
    faces = jnp.concatenate([diffusion, diffusion[-1:]])
    both = jnp.stack([faces[:-1], faces[:0:-1]])
    starts = jnp.broadcast_to(jnp.stack([faces[0], faces[-1]])[:, None], (2, count))
    ends = jnp.broadcast_to(jnp.stack([faces[-1], faces[0]])[:, None], (2, count))
    pad = ((0, 6), (0, 0))
    shape = jax.ShapeDtypeStruct((8, count), jnp.float32)
    values, totals = pl.pallas_call(prefix_kernel, out_shape=(shape, shape), name="green")(
        jnp.pad(1.0 / both, pad), jnp.pad(starts, pad), jnp.pad(ends, pad)
    )
    return values[0], values[1, ::-1], 1.0 / totals[0, count - 1]


def halos(shard, axis, dim):
    peers, length = lax.axis_size(axis), shard.shape[dim]
    last = lax.slice_in_dim(shard, length - 1, length, axis=dim)
    first = lax.slice_in_dim(shard, 0, 1, axis=dim)
    if peers == 2:
        both = lax.ppermute(jnp.concatenate([first, last], axis=dim), axis, [(0, 1), (1, 0)])
        return lax.slice_in_dim(both, 1, 2, axis=dim), lax.slice_in_dim(both, 0, 1, axis=dim)
    up = [(i, (i + 1) % peers) for i in range(peers)]
    return lax.ppermute(last, axis, up), lax.ppermute(first, axis, [(j, i) for i, j in up])


def difference(shard, sides, dim):
    before, after = sides
    length = shard.shape[dim]
    ahead = jnp.concatenate([lax.slice_in_dim(shard, 1, length, axis=dim), after], axis=dim)
    behind = jnp.concatenate([before, lax.slice_in_dim(shard, 0, length - 1, axis=dim)], axis=dim)
    return ahead - behind


def local(velocity, cotangent, in_weight, in_bias, out_weight, diffusion, stencil, wall_mask):
    line_count = lax.axis_size("line")
    line_index = lax.axis_index("line")
    _, row_count, planes, cells = velocity.shape
    columns = planes * cells
    hidden_count, feature_count = in_weight.shape
    share = hidden_count // line_count
    at_top = line_index == line_count - 1

    slab_bottom = velocity[:, :WALL_ROWS]
    slab_top = velocity[:, row_count - WALL_ROWS :][:, ::-1]
    own_slab = jnp.where(at_top, slab_top, slab_bottom).reshape(3 * WALL_ROWS, columns)
    slabs = lax.all_gather(own_slab, "line")
    walls = (slabs[0], slabs[line_count - 1])

    low, high, scale = green_factors(diffusion)
    all_rows = low.shape[0]
    low_own = lax.dynamic_slice_in_dim(low, line_index * row_count, row_count)
    high_own = lax.dynamic_slice_in_dim(high, line_index * row_count, row_count)
    rows = jnp.arange(row_count)
    green = (
        jnp.where(
            rows[:, None] >= rows[None, :],
            high_own[:, None] * low_own[None, :],
            low_own[:, None] * high_own[None, :],
        )
        * scale
    )
    operator = jnp.concatenate([green, low_own[None], high_own[None]])

    grad_stream = difference(velocity, halos(velocity, "stream", 3), 3)
    grad_span = difference(velocity, halos(velocity, "span", 2), 2)
    explicit = velocity - ADVECT * (velocity[0] * grad_stream + velocity[2] * grad_span)

    weight_in = lax.dynamic_slice_in_dim(in_weight, line_index * share, share, 0)
    bias_in = lax.dynamic_slice_in_dim(in_bias, line_index * share, share, 0)
    weight_out = lax.dynamic_slice_in_dim(out_weight, line_index * share, share, 1)
    slots = jnp.arange(3 * WALL_ROWS)
    pick = (stencil[:, :, None] == slots).astype(jnp.float32)
    features = jnp.concatenate(
        [
            jnp.dot(pick[w], walls[w], precision=HIGHEST)
            for w in range(2)
        ],
        axis=1,
    ).astype(jnp.bfloat16)
    hidden = jnp.tanh(
        jnp.dot(weight_in, features, preferred_element_type=jnp.float32) + bias_in[:, None]
    ).astype(jnp.bfloat16)
    stress_part = jnp.dot(weight_out, hidden, preferred_element_type=jnp.float32)

    both = jnp.concatenate([explicit, cotangent])
    solved = jnp.einsum("ij,cjzx->cizx", operator, both, precision=HIGHEST)
    sums = solved[:, row_count:].reshape(12, columns)
    stress_part = stress_part.reshape(3, 2, columns).reshape(6, columns)
    gathered = lax.all_gather(jnp.concatenate([sums, stress_part]), "line")
    part = gathered[:, :12].reshape(line_count, 6, 2, planes, cells)
    place = jnp.arange(line_count)
    below = (place < line_index).astype(jnp.float32)
    above = (place > line_index).astype(jnp.float32)
    sum_below = jnp.sum(part[:, :, 0] * below[:, None, None, None], axis=0) * scale
    sum_above = jnp.sum(part[:, :, 1] * above[:, None, None, None], axis=0) * scale
    mask_float = wall_mask.astype(jnp.float32)
    stress = jnp.sum(gathered[:, 12:], axis=0).reshape(3, 2, planes, cells) * mask_float[None]
    from_low = sum_below[:3] + stress[:, 0] * (low[0] * scale)
    from_high = sum_above[:3] + stress[:, 1] * (high[all_rows - 1] * scale)
    low_col, high_col = low_own[None, :, None, None], high_own[None, :, None, None]
    new_velocity = solved[:3, :row_count] + high_col * from_low[:, None] + low_col * from_high[:, None]
    multiplier = (
        solved[3:, :row_count] + high_col * sum_below[3:, None] + low_col * sum_above[3:, None]
    )

    wall_total = jnp.sum(part[:, 3:], axis=0)
    wall_multiplier = jnp.stack(
        [
            wall_total[:, 1] * (low[0] * scale),
            wall_total[:, 0] * (high[all_rows - 1] * scale),
        ],
        axis=1,
    )
    stress_grad = (wall_multiplier * mask_float[None]).astype(jnp.bfloat16).reshape(3, 2 * columns)
    hidden_grad = lax.dot_general(
        weight_out, stress_grad, (((0,), (0,)), ((), ())), preferred_element_type=jnp.float32
    )
    hidden_float = hidden.astype(jnp.float32)
    pre_grad = (hidden_grad * (1.0 - hidden_float * hidden_float)).astype(jnp.bfloat16)
    wide = jnp.concatenate([features, jnp.ones((1, 2 * columns), jnp.bfloat16)])
    grad_in = lax.dot_general(
        pre_grad, wide, (((1,), (1,)), ((), ())), preferred_element_type=jnp.float32
    )
    grad_out = lax.dot_general(
        hidden, stress_grad, (((1,), (1,)), ((), ())), preferred_element_type=jnp.float32
    )
    totals = lax.psum(jnp.concatenate([grad_in, grad_out], axis=1), ("stream", "span"))

    feature_grad = lax.dot_general(
        weight_in, pre_grad, (((0,), (0,)), ((), ())), preferred_element_type=jnp.float32
    )
    slab_part = jnp.stack(
        [
            lax.dot_general(
                pick[w],
                feature_grad[:, w * columns : (w + 1) * columns],
                (((0,), (0,)), ((), ())),
                precision=HIGHEST,
            )
            for w in range(2)
        ]
    )
    slab_sum = lax.psum(slab_part, "line")
    at_wall = jnp.logical_or(line_index == 0, at_top)
    slab_grad = jnp.where(at_top, slab_sum[1], slab_sum[0]) * at_wall.astype(jnp.float32)
    slab_grad = slab_grad.reshape(3, WALL_ROWS, planes, cells)

    flux_stream = velocity[0] * multiplier
    flux_span = velocity[2] * multiplier
    stream_diff = difference(flux_stream, halos(flux_stream, "stream", 3), 3)
    span_diff = difference(flux_span, halos(flux_span, "span", 2), 2)
    adjoint = multiplier + ADVECT * (stream_diff + span_diff)
    own = -ADVECT * jnp.stack(
        [
            jnp.sum(multiplier * grad_stream, axis=0),
            jnp.zeros(multiplier.shape[1:], jnp.float32),
            jnp.sum(multiplier * grad_span, axis=0),
        ]
    )
    edge = jnp.where(at_top, slab_grad[:, ::-1], slab_grad)
    rest = ((0, 0), (0, row_count - WALL_ROWS), (0, 0), (0, 0))
    rest_top = ((0, 0), (row_count - WALL_ROWS, 0), (0, 0), (0, 0))
    adjoint = adjoint + own + jnp.where(at_top, jnp.pad(edge, rest_top), jnp.pad(edge, rest))
    return (
        new_velocity,
        adjoint,
        totals[:, :feature_count],
        totals[:, feature_count],
        jnp.transpose(totals[:, feature_count + 1 :]),
    )


def solution(mesh):
    field = P(None, "line", "span", "stream")
    return jax.shard_map(
        local,
        mesh=mesh,
        in_specs=(field, field, P(), P(), P(), P(), P(), P(None, "span", "stream")),
        out_specs=(field, field, P("line", None), P("line"), P(None, "line")),
        check_vma=False,
    )
```

```python
import jax
import jax.numpy as jnp
from jax import lax
from jax.experimental import pallas as pl
from jax.experimental.pallas import tpu as pltpu
from jax.sharding import PartitionSpec as P

WALL_ROWS = 8
ADVECT = 0.2
HIGHEST = lax.Precision.HIGHEST


def prefix_kernel(step_ref, start_ref, end_ref, out_ref, total_ref):
    step = step_ref[...]
    count = step.shape[1]
    lane = lax.broadcasted_iota(jnp.int32, step.shape, 1)
    head = lane == 0
    one = jnp.ones_like(step)
    zero = jnp.zeros_like(step)
    a, b = one, jnp.where(head, zero, step)
    c, d = jnp.where(head, zero, one), jnp.where(head, one, one + step)
    hop = 1
    while hop < count:
        keep = lane >= hop
        pa = jnp.where(keep, pltpu.roll(a, hop, 1), one)
        pb = jnp.where(keep, pltpu.roll(b, hop, 1), zero)
        pc = jnp.where(keep, pltpu.roll(c, hop, 1), zero)
        pd = jnp.where(keep, pltpu.roll(d, hop, 1), one)
        a, b, c, d = a * pa + b * pc, a * pb + b * pd, c * pa + d * pc, c * pb + d * pd
        hop *= 2
    flux = start_ref[...] + 1.0
    value = a + b * flux
    out_ref[...] = value
    total_ref[...] = c + d * flux + end_ref[...] * value


MESH = pl.DeviceIdType.MESH
VMEM = pl.BlockSpec(memory_space=pltpu.VMEM)


def gather_kernel(count, part_ref, out_ref, slots, send_sem, recv_sem):
    me = lax.axis_index("line")
    barrier = pltpu.get_barrier_semaphore()
    for k in range(1, count):
        pl.semaphore_signal(
            barrier, inc=1, device_id={"line": lax.rem(me + k, count)}, device_id_type=MESH
        )
    pl.semaphore_wait(barrier, count - 1)
    copies = []
    for k in range(1, count):
        copy = pltpu.make_async_remote_copy(
            src_ref=part_ref,
            dst_ref=slots.at[k],
            send_sem=send_sem.at[k],
            recv_sem=recv_sem.at[k],
            device_id={"line": lax.rem(me + k, count)},
            device_id_type=MESH,
        )
        copy.start()
        copies.append(copy)
    out_ref[pl.ds(me, 1)] = part_ref[...][None]
    for k in range(1, count):
        copies[k - 1].wait_recv()
        out_ref[pl.ds(lax.rem(me + count - k, count), 1)] = slots[k][None]
    for copy in copies:
        copy.wait_send()


def line_gather(part, collective_id):
    count = lax.axis_size("line")
    return pl.pallas_call(
        lambda *refs: gather_kernel(count, *refs),
        out_shape=jax.ShapeDtypeStruct((count,) + part.shape, part.dtype),
        in_specs=[VMEM],
        out_specs=VMEM,
        scratch_shapes=[
            pltpu.VMEM((count,) + part.shape, part.dtype),
            pltpu.SemaphoreType.DMA((count,)),
            pltpu.SemaphoreType.DMA((count,)),
        ],
        compiler_params=pltpu.CompilerParams(
            collective_id=collective_id, has_side_effects=True, vmem_limit_bytes=32 * 2**20
        ),
        name="line_gather",
    )(part)


def sum_kernel(
    lines,
    streams,
    spans,
    part_ref,
    slab_ref,
    total_ref,
    wall_ref,
    arrived,
    whole,
    walls,
    scatter_send,
    scatter_recv,
    spread_send,
    spread_recv,
    wall_send,
    wall_recv,
):
    group = streams * spans
    chunk = part_ref.shape[0] // group
    line = lax.axis_index("line")
    me = lax.axis_index("stream") * spans + lax.axis_index("span")

    def member(k):
        other = lax.rem(me + k, group)
        return other, {"stream": other // spans, "span": lax.rem(other, spans)}

    def rows(index):
        return pl.ds(pl.multiple_of(index * chunk, 8), chunk)

    barrier = pltpu.get_barrier_semaphore()
    for k in range(1, group):
        pl.semaphore_signal(barrier, inc=1, device_id=member(k)[1], device_id_type=MESH)
    for k in range(1, lines):
        pl.semaphore_signal(
            barrier, inc=1, device_id={"line": lax.rem(line + k, lines)}, device_id_type=MESH
        )
    pl.semaphore_wait(barrier, group + lines - 2)

    scatter = []
    for k in range(1, group):
        other, device = member(k)
        copy = pltpu.make_async_remote_copy(
            src_ref=part_ref.at[rows(other)],
            dst_ref=arrived.at[k],
            send_sem=scatter_send.at[k],
            recv_sem=scatter_recv.at[k],
            device_id=device,
            device_id_type=MESH,
        )
        copy.start()
        scatter.append(copy)

    def wall_copy(wall, slot, target):
        return pltpu.make_async_remote_copy(
            src_ref=slab_ref.at[wall],
            dst_ref=walls.at[slot],
            send_sem=wall_send.at[wall],
            recv_sem=wall_recv.at[slot],
            device_id={"line": target},
            device_id_type=MESH,
        )

    ends = (0, lines - 1)
    for wall, target in enumerate(ends):

        @pl.when(line != target)
        def _(wall=wall, target=target):
            wall_copy(wall, lax.rem(line - target + lines, lines), target).start()

    own = part_ref[rows(me)]
    for k in range(1, group):
        scatter[k - 1].wait_recv()
        own = own + arrived[k]
    whole[rows(me)] = own
    spread = []
    for k in range(1, group):
        copy = pltpu.make_async_remote_copy(
            src_ref=whole.at[rows(me)],
            dst_ref=whole.at[rows(me)],
            send_sem=spread_send.at[k],
            recv_sem=spread_recv.at[k],
            device_id=member(k)[1],
            device_id_type=MESH,
        )
        copy.start()
        spread.append(copy)

    wall_ref[...] = jnp.zeros_like(wall_ref)
    for wall, target in enumerate(ends):

        @pl.when(line == target)
        def _(wall=wall, target=target):
            added = slab_ref[wall]
            for k in range(1, lines):
                wall_copy(wall, k, lax.rem(line + 1, lines)).wait_recv()
                added = added + walls[k]
            wall_ref[...] = added

        @pl.when(line != target)
        def _(wall=wall, target=target):
            wall_copy(wall, lax.rem(line - target + lines, lines), target).wait_send()

    for copy in spread:
        copy.wait_recv()
    total_ref[...] = whole[...]
    for copy in scatter + spread:
        copy.wait_send()


def group_sum(part, slabs):
    lines, streams, spans = (lax.axis_size(a) for a in ("line", "stream", "span"))
    group = streams * spans
    height = part.shape[0]
    padded = -(-height // (8 * group)) * (8 * group)
    part = jnp.pad(part, ((0, padded - height), (0, 0)))
    dma = pltpu.SemaphoreType.DMA
    total, wall = pl.pallas_call(
        lambda *refs: sum_kernel(lines, streams, spans, *refs),
        out_shape=(
            jax.ShapeDtypeStruct(part.shape, jnp.float32),
            jax.ShapeDtypeStruct(slabs.shape[1:], jnp.float32),
        ),
        in_specs=[VMEM, VMEM],
        out_specs=(VMEM, VMEM),
        scratch_shapes=[
            pltpu.VMEM((group, padded // group, part.shape[1]), jnp.float32),
            pltpu.VMEM(part.shape, jnp.float32),
            pltpu.VMEM((lines,) + slabs.shape[1:], jnp.float32),
            dma((group,)),
            dma((group,)),
            dma((group,)),
            dma((group,)),
            dma((2,)),
            dma((lines,)),
        ],
        compiler_params=pltpu.CompilerParams(
            collective_id=2, has_side_effects=True, vmem_limit_bytes=32 * 2**20
        ),
        name="group_sum",
    )(part, slabs)
    return total[:height], wall


def green_factors(diffusion):
    count = diffusion.shape[0]
    faces = jnp.concatenate([diffusion, diffusion[-1:]])
    both = jnp.stack([faces[:-1], faces[:0:-1]])
    starts = jnp.broadcast_to(jnp.stack([faces[0], faces[-1]])[:, None], (2, count))
    ends = jnp.broadcast_to(jnp.stack([faces[-1], faces[0]])[:, None], (2, count))
    pad = ((0, 6), (0, 0))
    shape = jax.ShapeDtypeStruct((8, count), jnp.float32)
    values, totals = pl.pallas_call(prefix_kernel, out_shape=(shape, shape), name="green")(
        jnp.pad(1.0 / both, pad), jnp.pad(starts, pad), jnp.pad(ends, pad)
    )
    return values[0], values[1, ::-1], 1.0 / totals[0, count - 1]


def halos(shard, axis, dim):
    peers, length = lax.axis_size(axis), shard.shape[dim]
    last = lax.slice_in_dim(shard, length - 1, length, axis=dim)
    first = lax.slice_in_dim(shard, 0, 1, axis=dim)
    if peers == 2:
        both = lax.ppermute(jnp.concatenate([first, last], axis=dim), axis, [(0, 1), (1, 0)])
        return lax.slice_in_dim(both, 1, 2, axis=dim), lax.slice_in_dim(both, 0, 1, axis=dim)
    up = [(i, (i + 1) % peers) for i in range(peers)]
    return lax.ppermute(last, axis, up), lax.ppermute(first, axis, [(j, i) for i, j in up])


def difference(shard, sides, dim):
    before, after = sides
    length = shard.shape[dim]
    ahead = jnp.concatenate([lax.slice_in_dim(shard, 1, length, axis=dim), after], axis=dim)
    behind = jnp.concatenate([before, lax.slice_in_dim(shard, 0, length - 1, axis=dim)], axis=dim)
    return ahead - behind


def local(velocity, cotangent, in_weight, in_bias, out_weight, diffusion, stencil, wall_mask):
    line_count = lax.axis_size("line")
    line_index = lax.axis_index("line")
    _, row_count, planes, cells = velocity.shape
    columns = planes * cells
    hidden_count, feature_count = in_weight.shape
    share = hidden_count // line_count
    at_top = line_index == line_count - 1

    slab_bottom = velocity[:, :WALL_ROWS]
    slab_top = velocity[:, row_count - WALL_ROWS :][:, ::-1]
    own_slab = jnp.where(at_top, slab_top, slab_bottom).reshape(3 * WALL_ROWS, columns)
    slabs = line_gather(own_slab, 0)
    walls = (slabs[0], slabs[line_count - 1])

    low, high, scale = green_factors(diffusion)
    all_rows = low.shape[0]
    low_own = lax.dynamic_slice_in_dim(low, line_index * row_count, row_count)
    high_own = lax.dynamic_slice_in_dim(high, line_index * row_count, row_count)
    rows = jnp.arange(row_count)
    green = (
        jnp.where(
            rows[:, None] >= rows[None, :],
            high_own[:, None] * low_own[None, :],
            low_own[:, None] * high_own[None, :],
        )
        * scale
    )
    operator = jnp.concatenate([green, low_own[None], high_own[None]])

    grad_stream = difference(velocity, halos(velocity, "stream", 3), 3)
    grad_span = difference(velocity, halos(velocity, "span", 2), 2)
    explicit = velocity - ADVECT * (velocity[0] * grad_stream + velocity[2] * grad_span)

    weight_in = lax.dynamic_slice_in_dim(in_weight, line_index * share, share, 0)
    bias_in = lax.dynamic_slice_in_dim(in_bias, line_index * share, share, 0)
    weight_out = lax.dynamic_slice_in_dim(out_weight, line_index * share, share, 1)
    slots = jnp.arange(3 * WALL_ROWS)
    pick = (stencil[:, :, None] == slots).astype(jnp.float32)
    features = jnp.concatenate(
        [
            jnp.dot(pick[w], walls[w], precision=HIGHEST)
            for w in range(2)
        ],
        axis=1,
    ).astype(jnp.bfloat16)
    hidden = jnp.tanh(
        jnp.dot(weight_in, features, preferred_element_type=jnp.float32) + bias_in[:, None]
    ).astype(jnp.bfloat16)
    stress_part = jnp.dot(weight_out, hidden, preferred_element_type=jnp.float32)

    both = jnp.concatenate([explicit, cotangent])
    solved = jnp.einsum("ij,cjzx->cizx", operator, both, precision=HIGHEST)
    sums = solved[:, row_count:].reshape(12, columns)
    stress_part = stress_part.reshape(3, 2, columns).reshape(6, columns)
    fill = jnp.zeros((6, columns), jnp.float32)
    gathered = line_gather(jnp.concatenate([sums, stress_part, fill]), 1)
    part = gathered[:, :12].reshape(line_count, 6, 2, planes, cells)
    place = jnp.arange(line_count)
    below = (place < line_index).astype(jnp.float32)
    above = (place > line_index).astype(jnp.float32)
    sum_below = jnp.sum(part[:, :, 0] * below[:, None, None, None], axis=0) * scale
    sum_above = jnp.sum(part[:, :, 1] * above[:, None, None, None], axis=0) * scale
    mask_float = wall_mask.astype(jnp.float32)
    stress = jnp.sum(gathered[:, 12:18], axis=0).reshape(3, 2, planes, cells) * mask_float[None]
    from_low = sum_below[:3] + stress[:, 0] * (low[0] * scale)
    from_high = sum_above[:3] + stress[:, 1] * (high[all_rows - 1] * scale)
    low_col, high_col = low_own[None, :, None, None], high_own[None, :, None, None]
    new_velocity = solved[:3, :row_count] + high_col * from_low[:, None] + low_col * from_high[:, None]
    multiplier = (
        solved[3:, :row_count] + high_col * sum_below[3:, None] + low_col * sum_above[3:, None]
    )

    wall_total = jnp.sum(part[:, 3:], axis=0)
    wall_multiplier = jnp.stack(
        [
            wall_total[:, 1] * (low[0] * scale),
            wall_total[:, 0] * (high[all_rows - 1] * scale),
        ],
        axis=1,
    )
    stress_grad = (wall_multiplier * mask_float[None]).astype(jnp.bfloat16).reshape(3, 2 * columns)
    hidden_grad = lax.dot_general(
        weight_out, stress_grad, (((0,), (0,)), ((), ())), preferred_element_type=jnp.float32
    )
    hidden_float = hidden.astype(jnp.float32)
    pre_grad = (hidden_grad * (1.0 - hidden_float * hidden_float)).astype(jnp.bfloat16)
    contract = (((1,), (1,)), ((), ()))
    grad_in = lax.dot_general(pre_grad, features, contract, preferred_element_type=jnp.float32)
    grad_out = lax.dot_general(stress_grad, hidden, contract, preferred_element_type=jnp.float32)
    ones = jnp.ones((1, 2 * columns), jnp.bfloat16)
    grad_bias = lax.dot_general(ones, pre_grad, contract, preferred_element_type=jnp.float32)
    extra = jnp.concatenate([grad_out, grad_bias, jnp.zeros((4, share), jnp.float32)])
    extra_rows = 8 * share // feature_count

    feature_grad = lax.dot_general(
        weight_in, pre_grad, (((0,), (0,)), ((), ())), preferred_element_type=jnp.float32
    )
    slab_part = jnp.stack(
        [
            lax.dot_general(
                pick[w],
                feature_grad[:, w * columns : (w + 1) * columns],
                (((0,), (0,)), ((), ())),
                precision=HIGHEST,
            )
            for w in range(2)
        ]
    )
    packed = jnp.concatenate([grad_in, extra.reshape(extra_rows, feature_count)])
    totals, slab_grad = group_sum(packed, slab_part)
    extra_total = totals[share:].reshape(8, share)
    slab_grad = slab_grad.reshape(3, WALL_ROWS, planes, cells)

    flux_stream = velocity[0] * multiplier
    flux_span = velocity[2] * multiplier
    stream_diff = difference(flux_stream, halos(flux_stream, "stream", 3), 3)
    span_diff = difference(flux_span, halos(flux_span, "span", 2), 2)
    adjoint = multiplier + ADVECT * (stream_diff + span_diff)
    own = -ADVECT * jnp.stack(
        [
            jnp.sum(multiplier * grad_stream, axis=0),
            jnp.zeros(multiplier.shape[1:], jnp.float32),
            jnp.sum(multiplier * grad_span, axis=0),
        ]
    )
    edge = jnp.where(at_top, slab_grad[:, ::-1], slab_grad)
    rest = ((0, 0), (0, row_count - WALL_ROWS), (0, 0), (0, 0))
    rest_top = ((0, 0), (row_count - WALL_ROWS, 0), (0, 0), (0, 0))
    adjoint = adjoint + own + jnp.where(at_top, jnp.pad(edge, rest_top), jnp.pad(edge, rest))
    return (
        new_velocity,
        adjoint,
        totals[:share],
        extra_total[3],
        extra_total[:3],
    )


def solution(mesh):
    field = P(None, "line", "span", "stream")
    return jax.shard_map(
        local,
        mesh=mesh,
        in_specs=(field, field, P(), P(), P(), P(), P(), P(None, "span", "stream")),
        out_specs=(field, field, P("line", None), P("line"), P(None, "line")),
        check_vma=False,
    )
```

```python
import jax
import jax.numpy as jnp
from jax import lax
from jax.experimental import pallas as pl
from jax.experimental.pallas import tpu as pltpu
from jax.sharding import PartitionSpec as P

WALL_ROWS = 8
ADVECT = 0.2
HIGHEST = lax.Precision.HIGHEST


def prefix_kernel(step_ref, start_ref, end_ref, out_ref, total_ref):
    step = step_ref[...]
    count = step.shape[1]
    lane = lax.broadcasted_iota(jnp.int32, step.shape, 1)
    head = lane == 0
    one = jnp.ones_like(step)
    zero = jnp.zeros_like(step)
    a, b = one, jnp.where(head, zero, step)
    c, d = jnp.where(head, zero, one), jnp.where(head, one, one + step)
    hop = 1
    while hop < count:
        keep = lane >= hop
        pa = jnp.where(keep, pltpu.roll(a, hop, 1), one)
        pb = jnp.where(keep, pltpu.roll(b, hop, 1), zero)
        pc = jnp.where(keep, pltpu.roll(c, hop, 1), zero)
        pd = jnp.where(keep, pltpu.roll(d, hop, 1), one)
        a, b, c, d = a * pa + b * pc, a * pb + b * pd, c * pa + d * pc, c * pb + d * pd
        hop *= 2
    flux = start_ref[...] + 1.0
    value = a + b * flux
    out_ref[...] = value
    total_ref[...] = c + d * flux + end_ref[...] * value


MESH = pl.DeviceIdType.MESH
VMEM = pl.BlockSpec(memory_space=pltpu.VMEM)


def gather_kernel(count, part_ref, out_ref, slots, send_sem, recv_sem):
    me = lax.axis_index("line")
    barrier = pltpu.get_barrier_semaphore()
    for k in range(1, count):
        pl.semaphore_signal(
            barrier, inc=1, device_id={"line": lax.rem(me + k, count)}, device_id_type=MESH
        )
    pl.semaphore_wait(barrier, count - 1)
    copies = []
    for k in range(1, count):
        copy = pltpu.make_async_remote_copy(
            src_ref=part_ref,
            dst_ref=slots.at[k],
            send_sem=send_sem.at[k],
            recv_sem=recv_sem.at[k],
            device_id={"line": lax.rem(me + k, count)},
            device_id_type=MESH,
        )
        copy.start()
        copies.append(copy)
    out_ref[pl.ds(me, 1)] = part_ref[...][None]
    for k in range(1, count):
        copies[k - 1].wait_recv()
        out_ref[pl.ds(lax.rem(me + count - k, count), 1)] = slots[k][None]
    for copy in copies:
        copy.wait_send()


def line_gather(part, collective_id):
    count = lax.axis_size("line")
    return pl.pallas_call(
        lambda *refs: gather_kernel(count, *refs),
        out_shape=jax.ShapeDtypeStruct((count,) + part.shape, part.dtype),
        in_specs=[VMEM],
        out_specs=VMEM,
        scratch_shapes=[
            pltpu.VMEM((count,) + part.shape, part.dtype),
            pltpu.SemaphoreType.DMA((count,)),
            pltpu.SemaphoreType.DMA((count,)),
        ],
        compiler_params=pltpu.CompilerParams(
            collective_id=collective_id, has_side_effects=True, vmem_limit_bytes=32 * 2**20
        ),
        name="line_gather",
    )(part)


def sum_kernel(
    lines,
    streams,
    spans,
    part_ref,
    slab_ref,
    total_ref,
    wall_ref,
    arrived,
    whole,
    walls,
    scatter_send,
    scatter_recv,
    spread_send,
    spread_recv,
    wall_send,
    wall_recv,
):
    group = streams * spans
    chunk = part_ref.shape[0] // group
    line = lax.axis_index("line")
    me = lax.axis_index("stream") * spans + lax.axis_index("span")

    def member(k):
        other = lax.rem(me + k, group)
        return other, {"stream": other // spans, "span": lax.rem(other, spans)}

    def rows(index):
        return pl.ds(pl.multiple_of(index * chunk, 8), chunk)

    barrier = pltpu.get_barrier_semaphore()
    for k in range(1, group):
        pl.semaphore_signal(barrier, inc=1, device_id=member(k)[1], device_id_type=MESH)
    for k in range(1, lines):
        pl.semaphore_signal(
            barrier, inc=1, device_id={"line": lax.rem(line + k, lines)}, device_id_type=MESH
        )
    pl.semaphore_wait(barrier, group + lines - 2)

    scatter = []
    for k in range(1, group):
        other, device = member(k)
        copy = pltpu.make_async_remote_copy(
            src_ref=part_ref.at[rows(other)],
            dst_ref=arrived.at[k],
            send_sem=scatter_send.at[k],
            recv_sem=scatter_recv.at[k],
            device_id=device,
            device_id_type=MESH,
        )
        copy.start()
        scatter.append(copy)

    def wall_copy(wall, slot, target):
        return pltpu.make_async_remote_copy(
            src_ref=slab_ref.at[wall],
            dst_ref=walls.at[slot],
            send_sem=wall_send.at[wall],
            recv_sem=wall_recv.at[slot],
            device_id={"line": target},
            device_id_type=MESH,
        )

    ends = (0, lines - 1)
    for wall, target in enumerate(ends):

        @pl.when(line != target)
        def _(wall=wall, target=target):
            wall_copy(wall, lax.rem(line - target + lines, lines), target).start()

    own = part_ref[rows(me)]
    for k in range(1, group):
        scatter[k - 1].wait_recv()
        own = own + arrived[k]
    whole[rows(me)] = own
    spread = []
    for k in range(1, group):
        copy = pltpu.make_async_remote_copy(
            src_ref=whole.at[rows(me)],
            dst_ref=whole.at[rows(me)],
            send_sem=spread_send.at[k],
            recv_sem=spread_recv.at[k],
            device_id=member(k)[1],
            device_id_type=MESH,
        )
        copy.start()
        spread.append(copy)

    wall_ref[...] = jnp.zeros_like(wall_ref)
    for wall, target in enumerate(ends):

        @pl.when(line == target)
        def _(wall=wall, target=target):
            added = slab_ref[wall]
            for k in range(1, lines):
                wall_copy(wall, k, lax.rem(line + 1, lines)).wait_recv()
                added = added + walls[k]
            wall_ref[...] = added

        @pl.when(line != target)
        def _(wall=wall, target=target):
            wall_copy(wall, lax.rem(line - target + lines, lines), target).wait_send()

    for copy in spread:
        copy.wait_recv()
    total_ref[...] = whole[...]
    for copy in scatter + spread:
        copy.wait_send()


def group_sum(part, slabs):
    lines, streams, spans = (lax.axis_size(a) for a in ("line", "stream", "span"))
    group = streams * spans
    height = part.shape[0]
    padded = -(-height // (8 * group)) * (8 * group)
    part = jnp.pad(part, ((0, padded - height), (0, 0)))
    dma = pltpu.SemaphoreType.DMA
    total, wall = pl.pallas_call(
        lambda *refs: sum_kernel(lines, streams, spans, *refs),
        out_shape=(
            jax.ShapeDtypeStruct(part.shape, jnp.float32),
            jax.ShapeDtypeStruct(slabs.shape[1:], jnp.float32),
        ),
        in_specs=[VMEM, VMEM],
        out_specs=(VMEM, VMEM),
        scratch_shapes=[
            pltpu.VMEM((group, padded // group, part.shape[1]), jnp.float32),
            pltpu.VMEM(part.shape, jnp.float32),
            pltpu.VMEM((lines,) + slabs.shape[1:], jnp.float32),
            dma((group,)),
            dma((group,)),
            dma((group,)),
            dma((group,)),
            dma((2,)),
            dma((lines,)),
        ],
        compiler_params=pltpu.CompilerParams(
            collective_id=2, has_side_effects=True, vmem_limit_bytes=32 * 2**20
        ),
        name="group_sum",
    )(part, slabs)
    return total[:height], wall


def exchange(streams, spans, stream_part, span_part, refs):
    edge_out, edge_in, plane_out, plane_in, spread, send_sem, recv_sem = refs
    cells = spread.shape[2]
    stream, span = lax.axis_index("stream"), lax.axis_index("span")
    right = {"stream": lax.rem(stream + 1, streams)}
    left = {"stream": lax.rem(stream + streams - 1, streams)}
    after = {"span": lax.rem(span + 1, spans)}
    before = {"span": lax.rem(span + spans - 1, spans)}
    barrier = pltpu.get_barrier_semaphore()
    for device in (right, left, after, before):
        pl.semaphore_signal(barrier, inc=1, device_id=device, device_id_type=MESH)

    def hot(height, first, second):
        row = lax.broadcasted_iota(jnp.int32, (height, cells), 0)
        lane = lax.broadcasted_iota(jnp.int32, (height, cells), 1)
        low = jnp.logical_and(row == first, lane == 0)
        high = jnp.logical_and(row == second, lane == cells - 1)
        return jnp.logical_or(low, high).astype(jnp.float32)

    for c in range(3):
        planes = span_part(c)
        plane_out[0, c] = planes[:, 0, :]
        plane_out[1, c] = planes[:, planes.shape[1] - 1, :]
        edge_out[c] = lax.dot_general(
            hot(8, 0, 1),
            stream_part(c).reshape(-1, cells),
            (((1,), (1,)), ((), ())),
            precision=HIGHEST,
            preferred_element_type=jnp.float32,
        )
    pl.semaphore_wait(barrier, 4)
    copies = []
    for k, (source, target, device) in enumerate(
        (
            (edge_out, edge_in.at[0], right),
            (edge_out, edge_in.at[1], left),
            (plane_out.at[1], plane_in.at[0], after),
            (plane_out.at[0], plane_in.at[1], before),
        )
    ):
        copy = pltpu.make_async_remote_copy(
            src_ref=source,
            dst_ref=target,
            send_sem=send_sem.at[k],
            recv_sem=recv_sem.at[k],
            device_id=device,
            device_id_type=MESH,
        )
        copy.start()
        copies.append(copy)
    for copy in copies:
        copy.wait()
    for c in range(3):
        spread[c] = lax.dot_general(
            jnp.concatenate([edge_in[0, c], edge_in[1, c]]),
            hot(16, 1, 8),
            (((0,), (0,)), ((), ())),
            precision=HIGHEST,
            preferred_element_type=jnp.float32,
        )


def stream_difference(part, edges):
    cells = part.shape[2]
    lane = lax.broadcasted_iota(jnp.int32, part.shape, 2)
    ahead = jnp.where(lane == cells - 1, edges, pltpu.roll(part, cells - 1, 2))
    return ahead - jnp.where(lane == 0, edges, pltpu.roll(part, 1, 2))


def span_difference(part, before, after):
    planes = part.shape[1]
    plane = lax.broadcasted_iota(jnp.int32, part.shape, 1)
    ahead = jnp.where(plane == planes - 1, after[:, None, :], pltpu.roll(part, planes - 1, 1))
    return ahead - jnp.where(plane == 0, before[:, None, :], pltpu.roll(part, 1, 1))


def explicit_kernel(streams, spans, v_ref, explicit_ref, gs_ref, gp_ref, *refs):
    exchange(streams, spans, lambda c: v_ref[c], lambda c: v_ref[c], refs)
    plane_in, spread = refs[3], refs[4]
    _, row_count, planes, cells = v_ref.shape

    @pl.loop(0, row_count // 8)
    def _(step):
        base = pl.multiple_of(step * 8, 8)
        rows = pl.ds(base, 8)
        flat = pl.ds(pl.multiple_of(base * planes, 8), 8 * planes)
        for c in range(3):
            part = v_ref[c, rows]
            gs = stream_difference(part, spread[c, flat].reshape(8, planes, cells))
            gp = span_difference(part, plane_in[0, c, rows], plane_in[1, c, rows])
            gs_ref[c, rows] = gs
            gp_ref[c, rows] = gp
            explicit_ref[c, rows] = part - ADVECT * (v_ref[0, rows] * gs + v_ref[2, rows] * gp)


def adjoint_kernel(lines, streams, spans, v_ref, m_ref, gs_ref, gp_ref, wall_ref, out_ref, *refs):
    exchange(
        streams, spans, lambda c: v_ref[0] * m_ref[c], lambda c: v_ref[2] * m_ref[c], refs
    )
    plane_in, spread = refs[3], refs[4]
    _, row_count, planes, cells = v_ref.shape

    @pl.loop(0, row_count // 8)
    def _(step):
        base = pl.multiple_of(step * 8, 8)
        rows = pl.ds(base, 8)
        flat = pl.ds(pl.multiple_of(base * planes, 8), 8 * planes)
        along, across = 0.0, 0.0
        for c in range(3):
            along = along + m_ref[c, rows] * gs_ref[c, rows]
            across = across + m_ref[c, rows] * gp_ref[c, rows]
        for c in range(3):
            m = m_ref[c, rows]
            edges = spread[c, flat].reshape(8, planes, cells)
            diff = stream_difference(v_ref[0, rows] * m, edges) + span_difference(
                v_ref[2, rows] * m, plane_in[0, c, rows], plane_in[1, c, rows]
            )
            if c == 0:
                diff = diff - along
            if c == 2:
                diff = diff - across
            out_ref[c, rows] = m + ADVECT * diff

    line = lax.axis_index("line")

    @pl.when(line == 0)
    def _():
        for c in range(3):
            for k in range(WALL_ROWS):
                out_ref[c, k] = out_ref[c, k] + wall_ref[c, k]

    @pl.when(line == lines - 1)
    def _():
        for c in range(3):
            for k in range(WALL_ROWS):
                out_ref[c, row_count - 1 - k] = out_ref[c, row_count - 1 - k] + wall_ref[c, k]


def halo_call(kernel, outs, collective_id, name, *args):
    shape = args[0].shape
    _, row_count, planes, cells = shape
    vmem, dma = pltpu.VMEM, pltpu.SemaphoreType.DMA
    full = jax.ShapeDtypeStruct(shape, jnp.float32)
    return pl.pallas_call(
        kernel,
        out_shape=(full,) * outs,
        in_specs=[VMEM] * len(args),
        out_specs=(VMEM,) * outs,
        scratch_shapes=[
            vmem((3, 8, row_count * planes), jnp.float32),
            vmem((2, 3, 8, row_count * planes), jnp.float32),
            vmem((2, 3, row_count, cells), jnp.float32),
            vmem((2, 3, row_count, cells), jnp.float32),
            vmem((3, row_count * planes, cells), jnp.float32),
            dma((4,)),
            dma((4,)),
        ],
        compiler_params=pltpu.CompilerParams(
            collective_id=collective_id, has_side_effects=True, vmem_limit_bytes=32 * 2**20
        ),
        name=name,
    )(*args)


def green_factors(diffusion):
    count = diffusion.shape[0]
    faces = jnp.concatenate([diffusion, diffusion[-1:]])
    both = jnp.stack([faces[:-1], faces[:0:-1]])
    starts = jnp.broadcast_to(jnp.stack([faces[0], faces[-1]])[:, None], (2, count))
    ends = jnp.broadcast_to(jnp.stack([faces[-1], faces[0]])[:, None], (2, count))
    pad = ((0, 6), (0, 0))
    shape = jax.ShapeDtypeStruct((8, count), jnp.float32)
    values, totals = pl.pallas_call(prefix_kernel, out_shape=(shape, shape), name="green")(
        jnp.pad(1.0 / both, pad), jnp.pad(starts, pad), jnp.pad(ends, pad)
    )
    return values[0], values[1, ::-1], 1.0 / totals[0, count - 1]


def local(velocity, cotangent, in_weight, in_bias, out_weight, diffusion, stencil, wall_mask):
    line_count = lax.axis_size("line")
    line_index = lax.axis_index("line")
    _, row_count, planes, cells = velocity.shape
    columns = planes * cells
    hidden_count, feature_count = in_weight.shape
    share = hidden_count // line_count
    at_top = line_index == line_count - 1

    slab_bottom = velocity[:, :WALL_ROWS]
    slab_top = velocity[:, row_count - WALL_ROWS :][:, ::-1]
    own_slab = jnp.where(at_top, slab_top, slab_bottom).reshape(3 * WALL_ROWS, columns)
    slabs = line_gather(own_slab, 0)
    walls = (slabs[0], slabs[line_count - 1])

    low, high, scale = green_factors(diffusion)
    all_rows = low.shape[0]
    low_own = lax.dynamic_slice_in_dim(low, line_index * row_count, row_count)
    high_own = lax.dynamic_slice_in_dim(high, line_index * row_count, row_count)
    rows = jnp.arange(row_count)
    green = (
        jnp.where(
            rows[:, None] >= rows[None, :],
            high_own[:, None] * low_own[None, :],
            low_own[:, None] * high_own[None, :],
        )
        * scale
    )
    operator = jnp.concatenate([green, low_own[None], high_own[None]])

    streams, spans = lax.axis_size("stream"), lax.axis_size("span")
    explicit, grad_stream, grad_span = halo_call(
        lambda *refs: explicit_kernel(streams, spans, *refs), 3, 3, "explicit", velocity
    )

    weight_in = lax.dynamic_slice_in_dim(in_weight, line_index * share, share, 0)
    bias_in = lax.dynamic_slice_in_dim(in_bias, line_index * share, share, 0)
    weight_out = lax.dynamic_slice_in_dim(out_weight, line_index * share, share, 1)
    slots = jnp.arange(3 * WALL_ROWS)
    pick = (stencil[:, :, None] == slots).astype(jnp.float32)
    features = jnp.concatenate(
        [
            jnp.dot(pick[w], walls[w], precision=HIGHEST)
            for w in range(2)
        ],
        axis=1,
    ).astype(jnp.bfloat16)
    hidden = jnp.tanh(
        jnp.dot(weight_in, features, preferred_element_type=jnp.float32) + bias_in[:, None]
    ).astype(jnp.bfloat16)
    stress_part = jnp.dot(weight_out, hidden, preferred_element_type=jnp.float32)

    both = jnp.concatenate([explicit, cotangent])
    solved = jnp.einsum("ij,cjzx->cizx", operator, both, precision=HIGHEST)
    sums = solved[:, row_count:].reshape(12, columns)
    stress_part = stress_part.reshape(3, 2, columns).reshape(6, columns)
    fill = jnp.zeros((6, columns), jnp.float32)
    gathered = line_gather(jnp.concatenate([sums, stress_part, fill]), 1)
    part = gathered[:, :12].reshape(line_count, 6, 2, planes, cells)
    place = jnp.arange(line_count)
    below = (place < line_index).astype(jnp.float32)
    above = (place > line_index).astype(jnp.float32)
    sum_below = jnp.sum(part[:, :, 0] * below[:, None, None, None], axis=0) * scale
    sum_above = jnp.sum(part[:, :, 1] * above[:, None, None, None], axis=0) * scale
    mask_float = wall_mask.astype(jnp.float32)
    stress = jnp.sum(gathered[:, 12:18], axis=0).reshape(3, 2, planes, cells) * mask_float[None]
    from_low = sum_below[:3] + stress[:, 0] * (low[0] * scale)
    from_high = sum_above[:3] + stress[:, 1] * (high[all_rows - 1] * scale)
    low_col, high_col = low_own[None, :, None, None], high_own[None, :, None, None]
    new_velocity = solved[:3, :row_count] + high_col * from_low[:, None] + low_col * from_high[:, None]
    multiplier = (
        solved[3:, :row_count] + high_col * sum_below[3:, None] + low_col * sum_above[3:, None]
    )

    wall_total = jnp.sum(part[:, 3:], axis=0)
    wall_multiplier = jnp.stack(
        [
            wall_total[:, 1] * (low[0] * scale),
            wall_total[:, 0] * (high[all_rows - 1] * scale),
        ],
        axis=1,
    )
    stress_grad = (wall_multiplier * mask_float[None]).astype(jnp.bfloat16).reshape(3, 2 * columns)
    hidden_grad = lax.dot_general(
        weight_out, stress_grad, (((0,), (0,)), ((), ())), preferred_element_type=jnp.float32
    )
    hidden_float = hidden.astype(jnp.float32)
    pre_grad = (hidden_grad * (1.0 - hidden_float * hidden_float)).astype(jnp.bfloat16)
    contract = (((1,), (1,)), ((), ()))
    grad_in = lax.dot_general(pre_grad, features, contract, preferred_element_type=jnp.float32)
    grad_out = lax.dot_general(stress_grad, hidden, contract, preferred_element_type=jnp.float32)
    ones = jnp.ones((1, 2 * columns), jnp.bfloat16)
    grad_bias = lax.dot_general(ones, pre_grad, contract, preferred_element_type=jnp.float32)
    extra = jnp.concatenate([grad_out, grad_bias, jnp.zeros((4, share), jnp.float32)])
    extra_rows = 8 * share // feature_count

    feature_grad = lax.dot_general(
        weight_in, pre_grad, (((0,), (0,)), ((), ())), preferred_element_type=jnp.float32
    )
    slab_part = jnp.stack(
        [
            lax.dot_general(
                pick[w],
                feature_grad[:, w * columns : (w + 1) * columns],
                (((0,), (0,)), ((), ())),
                precision=HIGHEST,
            )
            for w in range(2)
        ]
    )
    packed = jnp.concatenate([grad_in, extra.reshape(extra_rows, feature_count)])
    totals, slab_grad = group_sum(packed, slab_part)
    extra_total = totals[share:].reshape(8, share)
    slab_grad = slab_grad.reshape(3, WALL_ROWS, planes, cells)
    (adjoint,) = halo_call(
        lambda *refs: adjoint_kernel(line_count, streams, spans, *refs),
        1,
        4,
        "adjoint",
        velocity,
        multiplier,
        grad_stream,
        grad_span,
        slab_grad,
    )
    return (
        new_velocity,
        adjoint,
        totals[:share],
        extra_total[3],
        extra_total[:3],
    )


def solution(mesh):
    field = P(None, "line", "span", "stream")
    return jax.shard_map(
        local,
        mesh=mesh,
        in_specs=(field, field, P(), P(), P(), P(), P(), P(None, "span", "stream")),
        out_specs=(field, field, P("line", None), P("line"), P(None, "line")),
        check_vma=False,
    )
```

```python
import jax
import jax.numpy as jnp
from jax import lax
from jax.experimental import pallas as pl
from jax.experimental.pallas import tpu as pltpu
from jax.sharding import PartitionSpec as P

WALL_ROWS = 8
ADVECT = 0.2
HIGHEST = lax.Precision.HIGHEST


def running_product(step, head, hop_of, keep_of):
    one = jnp.ones_like(step)
    zero = jnp.zeros_like(step)
    a, b = one, jnp.where(head, zero, step)
    c, d = jnp.where(head, zero, one), jnp.where(head, one, one + step)
    hop = 1
    while hop < step.shape[1]:
        keep, turn = keep_of(hop), hop_of(hop)
        pa = jnp.where(keep, pltpu.roll(a, turn, 1), one)
        pb = jnp.where(keep, pltpu.roll(b, turn, 1), zero)
        pc = jnp.where(keep, pltpu.roll(c, turn, 1), zero)
        pd = jnp.where(keep, pltpu.roll(d, turn, 1), one)
        a, b, c, d = a * pa + b * pc, a * pb + b * pd, c * pa + d * pc, c * pb + d * pd
        hop *= 2
    return a, b, c, d


def factor_kernel(face_ref, low_ref, high_ref):
    count = face_ref.shape[1]
    face = jnp.broadcast_to(face_ref[...], (8, count))
    lane = lax.broadcasted_iota(jnp.int32, face.shape, 1)
    first, last = lane == 0, lane == count - 1

    def only(where, value):
        return jnp.sum(jnp.where(where, value, 0.0), axis=1, keepdims=True)

    step = 1.0 / face
    start, end = only(first, face), only(last, face)
    a, b, c, d = running_product(step, first, lambda h: h, lambda h: lane >= h)
    low = a + b * (start + 1.0)
    wronskian = only(last, c + d * (start + 1.0) + end * low)
    a, b, _, _ = running_product(
        pltpu.roll(step, count - 1, 1), last, lambda h: count - h, lambda h: lane < count - h
    )
    low_ref[...] = low / wronskian
    high_ref[...] = a + b * (end + 1.0)


MESH = pl.DeviceIdType.MESH
VMEM = pl.BlockSpec(memory_space=pltpu.VMEM)


def gather_kernel(count, part_ref, out_ref, slots, send_sem, recv_sem):
    me = lax.axis_index("line")
    barrier = pltpu.get_barrier_semaphore()
    for k in range(1, count):
        pl.semaphore_signal(
            barrier, inc=1, device_id={"line": lax.rem(me + k, count)}, device_id_type=MESH
        )
    pl.semaphore_wait(barrier, count - 1)
    copies = []
    for k in range(1, count):
        copy = pltpu.make_async_remote_copy(
            src_ref=part_ref,
            dst_ref=slots.at[k],
            send_sem=send_sem.at[k],
            recv_sem=recv_sem.at[k],
            device_id={"line": lax.rem(me + k, count)},
            device_id_type=MESH,
        )
        copy.start()
        copies.append(copy)
    out_ref[pl.ds(me, 1)] = part_ref[...][None]
    for k in range(1, count):
        copies[k - 1].wait_recv()
        out_ref[pl.ds(lax.rem(me + count - k, count), 1)] = slots[k][None]
    for copy in copies:
        copy.wait_send()


def line_gather(part, collective_id):
    count = lax.axis_size("line")
    return pl.pallas_call(
        lambda *refs: gather_kernel(count, *refs),
        out_shape=jax.ShapeDtypeStruct((count,) + part.shape, part.dtype),
        in_specs=[VMEM],
        out_specs=VMEM,
        scratch_shapes=[
            pltpu.VMEM((count,) + part.shape, part.dtype),
            pltpu.SemaphoreType.DMA((count,)),
            pltpu.SemaphoreType.DMA((count,)),
        ],
        compiler_params=pltpu.CompilerParams(
            collective_id=collective_id, has_side_effects=True, vmem_limit_bytes=32 * 2**20
        ),
        name="line_gather",
    )(part)


def sum_kernel(
    lines,
    streams,
    spans,
    part_ref,
    slab_ref,
    total_ref,
    wall_ref,
    arrived,
    whole,
    walls,
    scatter_send,
    scatter_recv,
    spread_send,
    spread_recv,
    wall_send,
    wall_recv,
):
    group = streams * spans
    chunk = part_ref.shape[0] // group
    line = lax.axis_index("line")
    me = lax.axis_index("stream") * spans + lax.axis_index("span")

    def member(k):
        other = lax.rem(me + k, group)
        return other, {"stream": other // spans, "span": lax.rem(other, spans)}

    def rows(index):
        return pl.ds(pl.multiple_of(index * chunk, 8), chunk)

    barrier = pltpu.get_barrier_semaphore()
    for k in range(1, group):
        pl.semaphore_signal(barrier, inc=1, device_id=member(k)[1], device_id_type=MESH)
    for k in range(1, lines):
        pl.semaphore_signal(
            barrier, inc=1, device_id={"line": lax.rem(line + k, lines)}, device_id_type=MESH
        )
    pl.semaphore_wait(barrier, group + lines - 2)

    scatter = []
    for k in range(1, group):
        other, device = member(k)
        copy = pltpu.make_async_remote_copy(
            src_ref=part_ref.at[rows(other)],
            dst_ref=arrived.at[k],
            send_sem=scatter_send.at[k],
            recv_sem=scatter_recv.at[k],
            device_id=device,
            device_id_type=MESH,
        )
        copy.start()
        scatter.append(copy)

    def wall_copy(wall, slot, target):
        return pltpu.make_async_remote_copy(
            src_ref=slab_ref.at[wall],
            dst_ref=walls.at[slot],
            send_sem=wall_send.at[wall],
            recv_sem=wall_recv.at[slot],
            device_id={"line": target},
            device_id_type=MESH,
        )

    ends = (0, lines - 1)
    for wall, target in enumerate(ends):

        @pl.when(line != target)
        def _(wall=wall, target=target):
            wall_copy(wall, lax.rem(line - target + lines, lines), target).start()

    own = part_ref[rows(me)]
    for k in range(1, group):
        scatter[k - 1].wait_recv()
        own = own + arrived[k]
    whole[rows(me)] = own
    spread = []
    for k in range(1, group):
        copy = pltpu.make_async_remote_copy(
            src_ref=whole.at[rows(me)],
            dst_ref=whole.at[rows(me)],
            send_sem=spread_send.at[k],
            recv_sem=spread_recv.at[k],
            device_id=member(k)[1],
            device_id_type=MESH,
        )
        copy.start()
        spread.append(copy)

    wall_ref[...] = jnp.zeros_like(wall_ref)
    for wall, target in enumerate(ends):

        @pl.when(line == target)
        def _(wall=wall, target=target):
            added = slab_ref[wall]
            for k in range(1, lines):
                wall_copy(wall, k, lax.rem(line + 1, lines)).wait_recv()
                added = added + walls[k]
            wall_ref[...] = added

        @pl.when(line != target)
        def _(wall=wall, target=target):
            wall_copy(wall, lax.rem(line - target + lines, lines), target).wait_send()

    for copy in spread:
        copy.wait_recv()
    total_ref[...] = whole[...]
    for copy in scatter + spread:
        copy.wait_send()


def group_sum(part, slabs):
    lines, streams, spans = (lax.axis_size(a) for a in ("line", "stream", "span"))
    group = streams * spans
    height = part.shape[0]
    padded = -(-height // (8 * group)) * (8 * group)
    part = jnp.pad(part, ((0, padded - height), (0, 0)))
    dma = pltpu.SemaphoreType.DMA
    total, wall = pl.pallas_call(
        lambda *refs: sum_kernel(lines, streams, spans, *refs),
        out_shape=(
            jax.ShapeDtypeStruct(part.shape, jnp.float32),
            jax.ShapeDtypeStruct(slabs.shape[1:], jnp.float32),
        ),
        in_specs=[VMEM, VMEM],
        out_specs=(VMEM, VMEM),
        scratch_shapes=[
            pltpu.VMEM((group, padded // group, part.shape[1]), jnp.float32),
            pltpu.VMEM(part.shape, jnp.float32),
            pltpu.VMEM((lines,) + slabs.shape[1:], jnp.float32),
            dma((group,)),
            dma((group,)),
            dma((group,)),
            dma((group,)),
            dma((2,)),
            dma((lines,)),
        ],
        compiler_params=pltpu.CompilerParams(
            collective_id=2, has_side_effects=True, vmem_limit_bytes=32 * 2**20
        ),
        name="group_sum",
    )(part, slabs)
    return total[:height], wall


def exchange(streams, spans, stream_part, span_part, refs):
    edge_out, edge_in, plane_out, plane_in, spread, send_sem, recv_sem = refs
    cells = spread.shape[2]
    stream, span = lax.axis_index("stream"), lax.axis_index("span")
    right = {"stream": lax.rem(stream + 1, streams)}
    left = {"stream": lax.rem(stream + streams - 1, streams)}
    after = {"span": lax.rem(span + 1, spans)}
    before = {"span": lax.rem(span + spans - 1, spans)}
    barrier = pltpu.get_barrier_semaphore()
    for device in (right, left, after, before):
        pl.semaphore_signal(barrier, inc=1, device_id=device, device_id_type=MESH)

    def hot(height, first, second):
        row = lax.broadcasted_iota(jnp.int32, (height, cells), 0)
        lane = lax.broadcasted_iota(jnp.int32, (height, cells), 1)
        low = jnp.logical_and(row == first, lane == 0)
        high = jnp.logical_and(row == second, lane == cells - 1)
        return jnp.logical_or(low, high).astype(jnp.float32)

    for c in range(3):
        planes = span_part(c)
        plane_out[0, c] = planes[:, 0, :]
        plane_out[1, c] = planes[:, planes.shape[1] - 1, :]
        edge_out[c] = lax.dot_general(
            hot(8, 0, 1),
            stream_part(c).reshape(-1, cells),
            (((1,), (1,)), ((), ())),
            precision=HIGHEST,
            preferred_element_type=jnp.float32,
        )
    pl.semaphore_wait(barrier, 4)
    copies = []
    for k, (source, target, device) in enumerate(
        (
            (edge_out, edge_in.at[0], right),
            (edge_out, edge_in.at[1], left),
            (plane_out.at[1], plane_in.at[0], after),
            (plane_out.at[0], plane_in.at[1], before),
        )
    ):
        copy = pltpu.make_async_remote_copy(
            src_ref=source,
            dst_ref=target,
            send_sem=send_sem.at[k],
            recv_sem=recv_sem.at[k],
            device_id=device,
            device_id_type=MESH,
        )
        copy.start()
        copies.append(copy)
    for copy in copies:
        copy.wait()
    for c in range(3):
        spread[c] = lax.dot_general(
            jnp.concatenate([edge_in[0, c], edge_in[1, c]]),
            hot(16, 1, 8),
            (((0,), (0,)), ((), ())),
            precision=HIGHEST,
            preferred_element_type=jnp.float32,
        )


def stream_difference(part, edges):
    cells = part.shape[2]
    lane = lax.broadcasted_iota(jnp.int32, part.shape, 2)
    ahead = jnp.where(lane == cells - 1, edges, pltpu.roll(part, cells - 1, 2))
    return ahead - jnp.where(lane == 0, edges, pltpu.roll(part, 1, 2))


def span_difference(part, before, after):
    planes = part.shape[1]
    plane = lax.broadcasted_iota(jnp.int32, part.shape, 1)
    ahead = jnp.where(plane == planes - 1, after[:, None, :], pltpu.roll(part, planes - 1, 1))
    return ahead - jnp.where(plane == 0, before[:, None, :], pltpu.roll(part, 1, 1))


def explicit_kernel(streams, spans, v_ref, explicit_ref, gs_ref, gp_ref, *refs):
    exchange(streams, spans, lambda c: v_ref[c], lambda c: v_ref[c], refs)
    plane_in, spread = refs[3], refs[4]
    _, row_count, planes, cells = v_ref.shape

    @pl.loop(0, row_count // 8)
    def _(step):
        base = pl.multiple_of(step * 8, 8)
        rows = pl.ds(base, 8)
        flat = pl.ds(pl.multiple_of(base * planes, 8), 8 * planes)
        for c in range(3):
            part = v_ref[c, rows]
            gs = stream_difference(part, spread[c, flat].reshape(8, planes, cells))
            gp = span_difference(part, plane_in[0, c, rows], plane_in[1, c, rows])
            gs_ref[c, rows] = gs
            gp_ref[c, rows] = gp
            explicit_ref[c, rows] = part - ADVECT * (v_ref[0, rows] * gs + v_ref[2, rows] * gp)


def adjoint_kernel(lines, streams, spans, v_ref, m_ref, gs_ref, gp_ref, wall_ref, out_ref, *refs):
    exchange(
        streams, spans, lambda c: v_ref[0] * m_ref[c], lambda c: v_ref[2] * m_ref[c], refs
    )
    plane_in, spread = refs[3], refs[4]
    _, row_count, planes, cells = v_ref.shape

    @pl.loop(0, row_count // 8)
    def _(step):
        base = pl.multiple_of(step * 8, 8)
        rows = pl.ds(base, 8)
        flat = pl.ds(pl.multiple_of(base * planes, 8), 8 * planes)
        along, across = 0.0, 0.0
        for c in range(3):
            along = along + m_ref[c, rows] * gs_ref[c, rows]
            across = across + m_ref[c, rows] * gp_ref[c, rows]
        for c in range(3):
            m = m_ref[c, rows]
            edges = spread[c, flat].reshape(8, planes, cells)
            diff = stream_difference(v_ref[0, rows] * m, edges) + span_difference(
                v_ref[2, rows] * m, plane_in[0, c, rows], plane_in[1, c, rows]
            )
            if c == 0:
                diff = diff - along
            if c == 2:
                diff = diff - across
            out_ref[c, rows] = m + ADVECT * diff

    line = lax.axis_index("line")

    @pl.when(line == 0)
    def _():
        for c in range(3):
            for k in range(WALL_ROWS):
                out_ref[c, k] = out_ref[c, k] + wall_ref[c, k]

    @pl.when(line == lines - 1)
    def _():
        for c in range(3):
            for k in range(WALL_ROWS):
                out_ref[c, row_count - 1 - k] = out_ref[c, row_count - 1 - k] + wall_ref[c, k]


def halo_call(kernel, outs, collective_id, name, *args):
    shape = args[0].shape
    _, row_count, planes, cells = shape
    vmem, dma = pltpu.VMEM, pltpu.SemaphoreType.DMA
    full = jax.ShapeDtypeStruct(shape, jnp.float32)
    return pl.pallas_call(
        kernel,
        out_shape=(full,) * outs,
        in_specs=[VMEM] * len(args),
        out_specs=(VMEM,) * outs,
        scratch_shapes=[
            vmem((3, 8, row_count * planes), jnp.float32),
            vmem((2, 3, 8, row_count * planes), jnp.float32),
            vmem((2, 3, row_count, cells), jnp.float32),
            vmem((2, 3, row_count, cells), jnp.float32),
            vmem((3, row_count * planes, cells), jnp.float32),
            dma((4,)),
            dma((4,)),
        ],
        compiler_params=pltpu.CompilerParams(
            collective_id=collective_id, has_side_effects=True, vmem_limit_bytes=32 * 2**20
        ),
        name=name,
    )(*args)


def green_factors(diffusion):
    count = diffusion.shape[0]
    shape = jax.ShapeDtypeStruct((8, count), jnp.float32)
    low, high = pl.pallas_call(factor_kernel, out_shape=(shape, shape), name="green")(
        diffusion.reshape(1, count)
    )
    return low[0], high[0]


def local(velocity, cotangent, in_weight, in_bias, out_weight, diffusion, stencil, wall_mask):
    line_count = lax.axis_size("line")
    line_index = lax.axis_index("line")
    _, row_count, planes, cells = velocity.shape
    columns = planes * cells
    hidden_count, feature_count = in_weight.shape
    share = hidden_count // line_count
    at_top = line_index == line_count - 1

    slab_bottom = velocity[:, :WALL_ROWS]
    slab_top = velocity[:, row_count - WALL_ROWS :][:, ::-1]
    own_slab = jnp.where(at_top, slab_top, slab_bottom).reshape(3 * WALL_ROWS, columns)
    slabs = line_gather(own_slab, 0)
    walls = (slabs[0], slabs[line_count - 1])

    low, high = green_factors(diffusion)
    all_rows = low.shape[0]
    low_own = lax.dynamic_slice_in_dim(low, line_index * row_count, row_count)
    high_own = lax.dynamic_slice_in_dim(high, line_index * row_count, row_count)
    rows = jnp.arange(row_count)
    green = jnp.where(
        rows[:, None] >= rows[None, :],
        high_own[:, None] * low_own[None, :],
        low_own[:, None] * high_own[None, :],
    )
    operator = jnp.concatenate([green, low_own[None], high_own[None]])

    streams, spans = lax.axis_size("stream"), lax.axis_size("span")
    explicit, grad_stream, grad_span = halo_call(
        lambda *refs: explicit_kernel(streams, spans, *refs), 3, 3, "explicit", velocity
    )

    weight_in = lax.dynamic_slice_in_dim(in_weight, line_index * share, share, 0)
    bias_in = lax.dynamic_slice_in_dim(in_bias, line_index * share, share, 0)
    weight_out = lax.dynamic_slice_in_dim(out_weight, line_index * share, share, 1)
    slots = jnp.arange(3 * WALL_ROWS)
    pick = (stencil[:, :, None] == slots).astype(jnp.float32)
    features = jnp.concatenate(
        [
            jnp.dot(pick[w], walls[w], precision=HIGHEST)
            for w in range(2)
        ],
        axis=1,
    ).astype(jnp.bfloat16)
    hidden = jnp.tanh(
        jnp.dot(weight_in, features, preferred_element_type=jnp.float32) + bias_in[:, None]
    ).astype(jnp.bfloat16)
    stress_part = jnp.dot(weight_out, hidden, preferred_element_type=jnp.float32)

    both = jnp.concatenate([explicit, cotangent])
    solved = jnp.einsum("ij,cjzx->cizx", operator, both, precision=HIGHEST)
    sums = solved[:, row_count:].reshape(12, columns)
    stress_part = stress_part.reshape(3, 2, columns).reshape(6, columns)
    fill = jnp.zeros((6, columns), jnp.float32)
    gathered = line_gather(jnp.concatenate([sums, stress_part, fill]), 1)
    part = gathered[:, :12].reshape(line_count, 6, 2, planes, cells)
    place = jnp.arange(line_count)
    below = (place < line_index).astype(jnp.float32)
    above = (place > line_index).astype(jnp.float32)
    sum_below = jnp.sum(part[:, :, 0] * below[:, None, None, None], axis=0)
    sum_above = jnp.sum(part[:, :, 1] * above[:, None, None, None], axis=0)
    mask_float = wall_mask.astype(jnp.float32)
    stress = jnp.sum(gathered[:, 12:18], axis=0).reshape(3, 2, planes, cells) * mask_float[None]
    from_low = sum_below[:3] + stress[:, 0] * low[0]
    from_high = sum_above[:3] + stress[:, 1] * high[all_rows - 1]
    low_col, high_col = low_own[None, :, None, None], high_own[None, :, None, None]
    new_velocity = solved[:3, :row_count] + high_col * from_low[:, None] + low_col * from_high[:, None]
    multiplier = (
        solved[3:, :row_count] + high_col * sum_below[3:, None] + low_col * sum_above[3:, None]
    )

    wall_total = jnp.sum(part[:, 3:], axis=0)
    wall_multiplier = jnp.stack(
        [
            wall_total[:, 1] * low[0],
            wall_total[:, 0] * high[all_rows - 1],
        ],
        axis=1,
    )
    stress_grad = (wall_multiplier * mask_float[None]).astype(jnp.bfloat16).reshape(3, 2 * columns)
    hidden_grad = lax.dot_general(
        weight_out, stress_grad, (((0,), (0,)), ((), ())), preferred_element_type=jnp.float32
    )
    hidden_float = hidden.astype(jnp.float32)
    pre_grad = (hidden_grad * (1.0 - hidden_float * hidden_float)).astype(jnp.bfloat16)
    contract = (((1,), (1,)), ((), ()))
    grad_in = lax.dot_general(pre_grad, features, contract, preferred_element_type=jnp.float32)
    grad_out = lax.dot_general(stress_grad, hidden, contract, preferred_element_type=jnp.float32)
    ones = jnp.ones((1, 2 * columns), jnp.bfloat16)
    grad_bias = lax.dot_general(ones, pre_grad, contract, preferred_element_type=jnp.float32)
    extra = jnp.concatenate([grad_out, grad_bias, jnp.zeros((4, share), jnp.float32)])
    extra_rows = 8 * share // feature_count

    feature_grad = lax.dot_general(
        weight_in, pre_grad, (((0,), (0,)), ((), ())), preferred_element_type=jnp.float32
    )
    slab_part = jnp.stack(
        [
            lax.dot_general(
                pick[w],
                feature_grad[:, w * columns : (w + 1) * columns],
                (((0,), (0,)), ((), ())),
                precision=HIGHEST,
            )
            for w in range(2)
        ]
    )
    packed = jnp.concatenate([grad_in, extra.reshape(extra_rows, feature_count)])
    totals, slab_grad = group_sum(packed, slab_part)
    extra_total = totals[share:].reshape(8, share)
    slab_grad = slab_grad.reshape(3, WALL_ROWS, planes, cells)
    (adjoint,) = halo_call(
        lambda *refs: adjoint_kernel(line_count, streams, spans, *refs),
        1,
        4,
        "adjoint",
        velocity,
        multiplier,
        grad_stream,
        grad_span,
        slab_grad,
    )
    return (
        new_velocity,
        adjoint,
        totals[:share],
        extra_total[3],
        extra_total[:3],
    )


def solution(mesh):
    field = P(None, "line", "span", "stream")
    return jax.shard_map(
        local,
        mesh=mesh,
        in_specs=(field, field, P(), P(), P(), P(), P(), P(None, "span", "stream")),
        out_specs=(field, field, P("line", None), P("line"), P(None, "line")),
        check_vma=False,
    )
```

```python
import jax
import jax.numpy as jnp
from jax import lax
from jax.experimental import pallas as pl
from jax.experimental.pallas import tpu as pltpu
from jax.sharding import PartitionSpec as P

WALL_ROWS = 8
ADVECT = 0.2
HIGHEST = lax.Precision.HIGHEST


def running_product(step, head, hop_of, keep_of):
    one = jnp.ones_like(step)
    zero = jnp.zeros_like(step)
    a, b = one, jnp.where(head, zero, step)
    c, d = jnp.where(head, zero, one), jnp.where(head, one, one + step)
    hop = 1
    while hop < step.shape[1]:
        keep, turn = keep_of(hop), hop_of(hop)
        pa = jnp.where(keep, pltpu.roll(a, turn, 1), one)
        pb = jnp.where(keep, pltpu.roll(b, turn, 1), zero)
        pc = jnp.where(keep, pltpu.roll(c, turn, 1), zero)
        pd = jnp.where(keep, pltpu.roll(d, turn, 1), one)
        a, b, c, d = a * pa + b * pc, a * pb + b * pd, c * pa + d * pc, c * pb + d * pd
        hop *= 2
    return a, b, c, d


def factor_kernel(face_ref, low_ref, high_ref):
    count = face_ref.shape[1]
    face = jnp.broadcast_to(face_ref[...], (8, count))
    lane = lax.broadcasted_iota(jnp.int32, face.shape, 1)
    first, last = lane == 0, lane == count - 1

    def only(where, value):
        return jnp.sum(jnp.where(where, value, 0.0), axis=1, keepdims=True)

    step = 1.0 / face
    start, end = only(first, face), only(last, face)
    a, b, c, d = running_product(step, first, lambda h: h, lambda h: lane >= h)
    low = a + b * (start + 1.0)
    wronskian = only(last, c + d * (start + 1.0) + end * low)
    a, b, _, _ = running_product(
        pltpu.roll(step, count - 1, 1), last, lambda h: count - h, lambda h: lane < count - h
    )
    low_ref[...] = low / wronskian
    high_ref[...] = a + b * (end + 1.0)


MESH = pl.DeviceIdType.MESH
VMEM = pl.BlockSpec(memory_space=pltpu.VMEM)


def gather_kernel(count, part_ref, out_ref, slots, send_sem, recv_sem):
    me = lax.axis_index("line")
    barrier = pltpu.get_barrier_semaphore()
    for k in range(1, count):
        pl.semaphore_signal(
            barrier, inc=1, device_id={"line": lax.rem(me + k, count)}, device_id_type=MESH
        )
    pl.semaphore_wait(barrier, count - 1)
    copies = []
    for k in range(1, count):
        copy = pltpu.make_async_remote_copy(
            src_ref=part_ref,
            dst_ref=slots.at[k],
            send_sem=send_sem.at[k],
            recv_sem=recv_sem.at[k],
            device_id={"line": lax.rem(me + k, count)},
            device_id_type=MESH,
        )
        copy.start()
        copies.append(copy)
    out_ref[pl.ds(me, 1)] = part_ref[...][None]
    for k in range(1, count):
        copies[k - 1].wait_recv()
        out_ref[pl.ds(lax.rem(me + count - k, count), 1)] = slots[k][None]
    for copy in copies:
        copy.wait_send()


def line_gather(part, collective_id):
    count = lax.axis_size("line")
    return pl.pallas_call(
        lambda *refs: gather_kernel(count, *refs),
        out_shape=jax.ShapeDtypeStruct((count,) + part.shape, part.dtype),
        in_specs=[VMEM],
        out_specs=VMEM,
        scratch_shapes=[
            pltpu.VMEM((count,) + part.shape, part.dtype),
            pltpu.SemaphoreType.DMA((count,)),
            pltpu.SemaphoreType.DMA((count,)),
        ],
        compiler_params=pltpu.CompilerParams(
            collective_id=collective_id, has_side_effects=True, vmem_limit_bytes=32 * 2**20
        ),
        name="line_gather",
    )(part)


def sum_kernel(
    lines,
    streams,
    spans,
    part_ref,
    slab_ref,
    total_ref,
    wall_ref,
    arrived,
    whole,
    walls,
    scatter_send,
    scatter_recv,
    spread_send,
    spread_recv,
    wall_send,
    wall_recv,
):
    group = streams * spans
    chunk = part_ref.shape[0] // group
    line = lax.axis_index("line")
    me = lax.axis_index("stream") * spans + lax.axis_index("span")

    def member(k):
        other = lax.rem(me + k, group)
        return other, {"stream": other // spans, "span": lax.rem(other, spans)}

    def rows(index):
        return pl.ds(pl.multiple_of(index * chunk, 8), chunk)

    barrier = pltpu.get_barrier_semaphore()
    for k in range(1, group):
        pl.semaphore_signal(barrier, inc=1, device_id=member(k)[1], device_id_type=MESH)
    for k in range(1, lines):
        pl.semaphore_signal(
            barrier, inc=1, device_id={"line": lax.rem(line + k, lines)}, device_id_type=MESH
        )
    pl.semaphore_wait(barrier, group + lines - 2)

    scatter = []
    for k in range(1, group):
        other, device = member(k)
        copy = pltpu.make_async_remote_copy(
            src_ref=part_ref.at[rows(other)],
            dst_ref=arrived.at[k],
            send_sem=scatter_send.at[k],
            recv_sem=scatter_recv.at[k],
            device_id=device,
            device_id_type=MESH,
        )
        copy.start()
        scatter.append(copy)

    def wall_copy(wall, slot, target):
        return pltpu.make_async_remote_copy(
            src_ref=slab_ref.at[wall],
            dst_ref=walls.at[slot],
            send_sem=wall_send.at[wall],
            recv_sem=wall_recv.at[slot],
            device_id={"line": target},
            device_id_type=MESH,
        )

    ends = (0, lines - 1)
    for wall, target in enumerate(ends):

        @pl.when(line != target)
        def _(wall=wall, target=target):
            wall_copy(wall, lax.rem(line - target + lines, lines), target).start()

    own = part_ref[rows(me)]
    for k in range(1, group):
        scatter[k - 1].wait_recv()
        own = own + arrived[k]
    whole[rows(me)] = own
    spread = []
    for k in range(1, group):
        copy = pltpu.make_async_remote_copy(
            src_ref=whole.at[rows(me)],
            dst_ref=whole.at[rows(me)],
            send_sem=spread_send.at[k],
            recv_sem=spread_recv.at[k],
            device_id=member(k)[1],
            device_id_type=MESH,
        )
        copy.start()
        spread.append(copy)

    wall_ref[...] = jnp.zeros_like(wall_ref)
    for wall, target in enumerate(ends):

        @pl.when(line == target)
        def _(wall=wall, target=target):
            added = slab_ref[wall]
            for k in range(1, lines):
                wall_copy(wall, k, lax.rem(line + 1, lines)).wait_recv()
                added = added + walls[k]
            wall_ref[...] = added

        @pl.when(line != target)
        def _(wall=wall, target=target):
            wall_copy(wall, lax.rem(line - target + lines, lines), target).wait_send()

    for copy in spread:
        copy.wait_recv()
    total_ref[...] = whole[...]
    for copy in scatter + spread:
        copy.wait_send()


def group_sum(part, slabs):
    lines, streams, spans = (lax.axis_size(a) for a in ("line", "stream", "span"))
    group = streams * spans
    height = part.shape[0]
    padded = -(-height // (8 * group)) * (8 * group)
    part = jnp.pad(part, ((0, padded - height), (0, 0)))
    dma = pltpu.SemaphoreType.DMA
    total, wall = pl.pallas_call(
        lambda *refs: sum_kernel(lines, streams, spans, *refs),
        out_shape=(
            jax.ShapeDtypeStruct(part.shape, jnp.float32),
            jax.ShapeDtypeStruct(slabs.shape[1:], jnp.float32),
        ),
        in_specs=[VMEM, VMEM],
        out_specs=(VMEM, VMEM),
        scratch_shapes=[
            pltpu.VMEM((group, padded // group, part.shape[1]), jnp.float32),
            pltpu.VMEM(part.shape, jnp.float32),
            pltpu.VMEM((lines,) + slabs.shape[1:], jnp.float32),
            dma((group,)),
            dma((group,)),
            dma((group,)),
            dma((group,)),
            dma((2,)),
            dma((lines,)),
        ],
        compiler_params=pltpu.CompilerParams(
            collective_id=2, has_side_effects=True, vmem_limit_bytes=32 * 2**20
        ),
        name="group_sum",
    )(part, slabs)
    return total[:height], wall


def exchange(streams, spans, stream_part, span_part, refs):
    edge_out, edge_in, plane_out, plane_in, spread, send_sem, recv_sem = refs
    cells = spread.shape[2]
    stream, span = lax.axis_index("stream"), lax.axis_index("span")
    right = {"stream": lax.rem(stream + 1, streams)}
    left = {"stream": lax.rem(stream + streams - 1, streams)}
    after = {"span": lax.rem(span + 1, spans)}
    before = {"span": lax.rem(span + spans - 1, spans)}
    barrier = pltpu.get_barrier_semaphore()
    for device in (right, left, after, before):
        pl.semaphore_signal(barrier, inc=1, device_id=device, device_id_type=MESH)

    def hot(height, first, second):
        row = lax.broadcasted_iota(jnp.int32, (height, cells), 0)
        lane = lax.broadcasted_iota(jnp.int32, (height, cells), 1)
        low = jnp.logical_and(row == first, lane == 0)
        high = jnp.logical_and(row == second, lane == cells - 1)
        return jnp.logical_or(low, high).astype(jnp.float32)

    def send(k, source, target, device):
        copy = pltpu.make_async_remote_copy(
            src_ref=source,
            dst_ref=target,
            send_sem=send_sem.at[k],
            recv_sem=recv_sem.at[k],
            device_id=device,
            device_id_type=MESH,
        )
        copy.start()
        return copy

    for c in range(3):
        planes = span_part(c)
        plane_out[0, c] = planes[:, 0, :]
        plane_out[1, c] = planes[:, planes.shape[1] - 1, :]
    pl.semaphore_wait(barrier, 4)
    copies = [
        send(0, plane_out.at[1], plane_in.at[0], after),
        send(1, plane_out.at[0], plane_in.at[1], before),
    ]
    for c in range(3):
        edge_out[c] = lax.dot_general(
            hot(8, 0, 1),
            stream_part(c).reshape(-1, cells),
            (((1,), (1,)), ((), ())),
            precision=HIGHEST,
            preferred_element_type=jnp.float32,
        )
    copies += [send(2, edge_out, edge_in.at[0], right), send(3, edge_out, edge_in.at[1], left)]
    for copy in copies:
        copy.wait()
    for c in range(3):
        spread[c] = lax.dot_general(
            jnp.concatenate([edge_in[0, c], edge_in[1, c]]),
            hot(16, 1, 8),
            (((0,), (0,)), ((), ())),
            precision=HIGHEST,
            preferred_element_type=jnp.float32,
        )


def stream_difference(part, edges):
    cells = part.shape[2]
    lane = lax.broadcasted_iota(jnp.int32, part.shape, 2)
    ahead = jnp.where(lane == cells - 1, edges, pltpu.roll(part, cells - 1, 2))
    return ahead - jnp.where(lane == 0, edges, pltpu.roll(part, 1, 2))


def span_difference(part, before, after):
    planes = part.shape[1]
    plane = lax.broadcasted_iota(jnp.int32, part.shape, 1)
    ahead = jnp.where(plane == planes - 1, after[:, None, :], pltpu.roll(part, planes - 1, 1))
    return ahead - jnp.where(plane == 0, before[:, None, :], pltpu.roll(part, 1, 1))


def explicit_kernel(streams, spans, v_ref, explicit_ref, gs_ref, gp_ref, *refs):
    exchange(streams, spans, lambda c: v_ref[c], lambda c: v_ref[c], refs)
    plane_in, spread = refs[3], refs[4]
    _, row_count, planes, cells = v_ref.shape

    @pl.loop(0, row_count // 8)
    def _(step):
        base = pl.multiple_of(step * 8, 8)
        rows = pl.ds(base, 8)
        flat = pl.ds(pl.multiple_of(base * planes, 8), 8 * planes)
        for c in range(3):
            part = v_ref[c, rows]
            gs = stream_difference(part, spread[c, flat].reshape(8, planes, cells))
            gp = span_difference(part, plane_in[0, c, rows], plane_in[1, c, rows])
            gs_ref[c, rows] = gs
            gp_ref[c, rows] = gp
            explicit_ref[c, rows] = part - ADVECT * (v_ref[0, rows] * gs + v_ref[2, rows] * gp)


def adjoint_kernel(lines, streams, spans, v_ref, m_ref, gs_ref, gp_ref, wall_ref, out_ref, *refs):
    exchange(
        streams, spans, lambda c: v_ref[0] * m_ref[c], lambda c: v_ref[2] * m_ref[c], refs
    )
    plane_in, spread = refs[3], refs[4]
    _, row_count, planes, cells = v_ref.shape

    @pl.loop(0, row_count // 8)
    def _(step):
        base = pl.multiple_of(step * 8, 8)
        rows = pl.ds(base, 8)
        flat = pl.ds(pl.multiple_of(base * planes, 8), 8 * planes)
        along, across = 0.0, 0.0
        for c in range(3):
            along = along + m_ref[c, rows] * gs_ref[c, rows]
            across = across + m_ref[c, rows] * gp_ref[c, rows]
        for c in range(3):
            m = m_ref[c, rows]
            edges = spread[c, flat].reshape(8, planes, cells)
            diff = stream_difference(v_ref[0, rows] * m, edges) + span_difference(
                v_ref[2, rows] * m, plane_in[0, c, rows], plane_in[1, c, rows]
            )
            if c == 0:
                diff = diff - along
            if c == 2:
                diff = diff - across
            out_ref[c, rows] = m + ADVECT * diff

    line = lax.axis_index("line")

    @pl.when(line == 0)
    def _():
        for c in range(3):
            for k in range(WALL_ROWS):
                out_ref[c, k] = out_ref[c, k] + wall_ref[c, k]

    @pl.when(line == lines - 1)
    def _():
        for c in range(3):
            for k in range(WALL_ROWS):
                out_ref[c, row_count - 1 - k] = out_ref[c, row_count - 1 - k] + wall_ref[c, k]


def halo_call(kernel, outs, collective_id, name, *args):
    shape = args[0].shape
    _, row_count, planes, cells = shape
    vmem, dma = pltpu.VMEM, pltpu.SemaphoreType.DMA
    full = jax.ShapeDtypeStruct(shape, jnp.float32)
    return pl.pallas_call(
        kernel,
        out_shape=(full,) * outs,
        in_specs=[VMEM] * len(args),
        out_specs=(VMEM,) * outs,
        scratch_shapes=[
            vmem((3, 8, row_count * planes), jnp.float32),
            vmem((2, 3, 8, row_count * planes), jnp.float32),
            vmem((2, 3, row_count, cells), jnp.float32),
            vmem((2, 3, row_count, cells), jnp.float32),
            vmem((3, row_count * planes, cells), jnp.float32),
            dma((4,)),
            dma((4,)),
        ],
        compiler_params=pltpu.CompilerParams(
            collective_id=collective_id, has_side_effects=True, vmem_limit_bytes=32 * 2**20
        ),
        name=name,
    )(*args)


def green_factors(diffusion):
    count = diffusion.shape[0]
    shape = jax.ShapeDtypeStruct((8, count), jnp.float32)
    low, high = pl.pallas_call(factor_kernel, out_shape=(shape, shape), name="green")(
        diffusion.reshape(1, count)
    )
    return low[0], high[0]


def local(velocity, cotangent, in_weight, in_bias, out_weight, diffusion, stencil, wall_mask):
    line_count = lax.axis_size("line")
    line_index = lax.axis_index("line")
    _, row_count, planes, cells = velocity.shape
    columns = planes * cells
    hidden_count, feature_count = in_weight.shape
    share = hidden_count // line_count
    at_top = line_index == line_count - 1

    slab_bottom = velocity[:, :WALL_ROWS]
    slab_top = velocity[:, row_count - WALL_ROWS :][:, ::-1]
    own_slab = jnp.where(at_top, slab_top, slab_bottom).reshape(3 * WALL_ROWS, columns)
    slabs = line_gather(own_slab, 0)
    walls = (slabs[0], slabs[line_count - 1])

    low, high = green_factors(diffusion)
    low_own = lax.dynamic_slice_in_dim(low, line_index * row_count, row_count)
    high_own = lax.dynamic_slice_in_dim(high, line_index * row_count, row_count)
    rows = jnp.arange(row_count)
    green = jnp.where(
        rows[:, None] >= rows[None, :],
        high_own[:, None] * low_own[None, :],
        low_own[:, None] * high_own[None, :],
    )
    operator = jnp.concatenate([green, low_own[None], high_own[None]])

    streams, spans = lax.axis_size("stream"), lax.axis_size("span")
    explicit, grad_stream, grad_span = halo_call(
        lambda *refs: explicit_kernel(streams, spans, *refs), 3, 3, "explicit", velocity
    )

    weight_in = lax.dynamic_slice_in_dim(in_weight, line_index * share, share, 0)
    bias_in = lax.dynamic_slice_in_dim(in_bias, line_index * share, share, 0)
    weight_out = lax.dynamic_slice_in_dim(out_weight, line_index * share, share, 1)
    slots = jnp.arange(3 * WALL_ROWS)
    pick = (stencil[:, :, None] == slots).astype(jnp.float32)
    features = jnp.concatenate(
        [
            jnp.dot(pick[w], walls[w], precision=HIGHEST)
            for w in range(2)
        ],
        axis=1,
    ).astype(jnp.bfloat16)
    hidden = jnp.tanh(
        jnp.dot(weight_in, features, preferred_element_type=jnp.float32) + bias_in[:, None]
    ).astype(jnp.bfloat16)
    stress_part = jnp.dot(weight_out, hidden, preferred_element_type=jnp.float32)

    both = jnp.concatenate([explicit, cotangent])
    solved = jnp.einsum("ij,cjzx->cizx", operator, both, precision=HIGHEST)
    sums = solved[:, row_count:].reshape(12, columns)
    stress_part = stress_part.reshape(3, 2, columns).reshape(6, columns)
    fill = jnp.zeros((6, columns), jnp.float32)
    gathered = line_gather(jnp.concatenate([sums, stress_part, fill]), 1)
    part = gathered[:, :12].reshape(line_count, 6, 2, planes, cells)
    place = jnp.arange(line_count)
    below = (place < line_index).astype(jnp.float32)
    above = (place > line_index).astype(jnp.float32)
    sum_below = jnp.sum(part[:, :, 0] * below[:, None, None, None], axis=0)
    sum_above = jnp.sum(part[:, :, 1] * above[:, None, None, None], axis=0)
    mask_float = wall_mask.astype(jnp.float32)
    stress = jnp.sum(gathered[:, 12:18], axis=0).reshape(3, 2, planes, cells) * mask_float[None]
    from_low = sum_below[:3] + stress[:, 0] * low[0]
    from_high = sum_above[:3] + stress[:, 1]
    low_col, high_col = low_own[None, :, None, None], high_own[None, :, None, None]
    new_velocity = solved[:3, :row_count] + high_col * from_low[:, None] + low_col * from_high[:, None]
    multiplier = (
        solved[3:, :row_count] + high_col * sum_below[3:, None] + low_col * sum_above[3:, None]
    )

    wall_total = jnp.sum(part[:, 3:], axis=0)
    wall_multiplier = jnp.stack(
        [
            wall_total[:, 1] * low[0],
            wall_total[:, 0],
        ],
        axis=1,
    )
    stress_grad = (wall_multiplier * mask_float[None]).astype(jnp.bfloat16).reshape(3, 2 * columns)
    hidden_grad = lax.dot_general(
        weight_out, stress_grad, (((0,), (0,)), ((), ())), preferred_element_type=jnp.float32
    )
    hidden_float = hidden.astype(jnp.float32)
    pre_grad = (hidden_grad * (1.0 - hidden_float * hidden_float)).astype(jnp.bfloat16)
    contract = (((1,), (1,)), ((), ()))
    grad_in = lax.dot_general(pre_grad, features, contract, preferred_element_type=jnp.float32)
    grad_out = lax.dot_general(stress_grad, hidden, contract, preferred_element_type=jnp.float32)
    ones = jnp.ones((1, 2 * columns), jnp.bfloat16)
    grad_bias = lax.dot_general(ones, pre_grad, contract, preferred_element_type=jnp.float32)
    extra = jnp.concatenate([grad_out, grad_bias, jnp.zeros((4, share), jnp.float32)])
    extra_rows = 8 * share // feature_count

    feature_grad = lax.dot_general(
        weight_in, pre_grad, (((0,), (0,)), ((), ())), preferred_element_type=jnp.float32
    )
    slab_part = jnp.stack(
        [
            lax.dot_general(
                pick[w],
                feature_grad[:, w * columns : (w + 1) * columns],
                (((0,), (0,)), ((), ())),
                precision=HIGHEST,
            )
            for w in range(2)
        ]
    )
    packed = jnp.concatenate([grad_in, extra.reshape(extra_rows, feature_count)])
    totals, slab_grad = group_sum(packed, slab_part)
    extra_total = totals[share:].reshape(8, share)
    slab_grad = slab_grad.reshape(3, WALL_ROWS, planes, cells)
    (adjoint,) = halo_call(
        lambda *refs: adjoint_kernel(line_count, streams, spans, *refs),
        1,
        4,
        "adjoint",
        velocity,
        multiplier,
        grad_stream,
        grad_span,
        slab_grad,
    )
    return (
        new_velocity,
        adjoint,
        totals[:share],
        extra_total[3],
        extra_total[:3],
    )


def solution(mesh):
    field = P(None, "line", "span", "stream")
    return jax.shard_map(
        local,
        mesh=mesh,
        in_specs=(field, field, P(), P(), P(), P(), P(), P(None, "span", "stream")),
        out_specs=(field, field, P("line", None), P("line"), P(None, "line")),
        check_vma=False,
    )
```
